1024 devices in a mesh: dp: 8 (over x, core), expert: 32 (over y, z_lo), tensor: 4 (over z_hi).
Axes of the slice: x: 4, y: 4, z: 32 (z_hi: 4, z_lo: 8; z = z_hi * 8 + z_lo), core: 2. Of those that a mesh axis runs over, the one named last changes fastest.
Arguments:
- cotangent: bfloat16 [14336, 4096], P(('dp', 'expert', 'tensor')), may hold values from -6 to 6
- probs: float32 [14336, 2], P(('dp', 'expert', 'tensor')), may hold values from 0.1 to 1
- expert_ids: int32 [14336, 2], P(('dp', 'expert')), may hold values from 0 to 15, all different within a row; in each aligned block of 56 rows (0 to 55, 56 to 111, ...) at most 8 rows name the same one
- saved_hidden: bfloat16 [2048, 51200], P('dp', ('expert', 'tensor')), may hold values from -0.29882812 to 0.29882812
- down_weight: bfloat16 [4096, 51200], P(None, ('expert', 'tensor')), may hold values from -0.09375 to 0.09375
Outputs:
- hidden_grad: bfloat16 [2048, 51200], P('dp', ('expert', 'tensor'))
- weight_grad: bfloat16 [4096, 51200], P('dp', ('expert', 'tensor'))
- prob_grad: float32 [14336, 2], P(('dp', 'expert', 'tensor'))
The draws below stay inside these ranges and needn't reach their ends.
Inputs may be any that keep to these rules, and one draw needn't show every extreme that they name: `expert_ids`: in each aligned block of 56 rows (one token group) no expert is named by more than 8 rows, a bound that some block reaches; the two ids of a row differ.
All inputs are finite; a program needn't handle non-finite values.
Results may differ from the reference program's by a relative error of at most 0.017.
Values may be sent and summed in bfloat16 or wider, within the bound.
No kernel may reach another device: no remote copies, remote signals or barrier semaphores. Data moves between devices by JAX's collectives and lax.ppermute only.
A program may use at most 32 MiB of HBM per device.

```python
import math
import jax
import jax.numpy as jnp
import numpy as np
from jax import lax

D = 4096
FF = 3200
TOP = 2
EXPERTS = 16
GROUP = 56
CAP = 8
TOKENS = 14336
N_DP = 8
N_EXPERT = 32


def block_levels(own_key, extent, cuts, least, largest):
    gain, own = 1.0, jax.random.fold_in(own_key, 6)
    for axis_at, shards_of in cuts:
        heights = jnp.exp(jax.random.uniform(jax.random.fold_in(own, axis_at), (shards_of,), jnp.float32, least / len(cuts), largest / len(cuts)))
        gain = gain * jnp.repeat(heights, extent[axis_at] // shards_of).reshape([-1 if axis == axis_at else 1 for axis in range(len(extent))])
    return gain


def deal_out(own_key, own, number, rows, number_of, top, most, lean):
    order = jax.random.permutation(own_key, number_of)
    packed, usual = shares(number_of, rows * top, most, lean, True), shares(number_of, rows * top, most, lean, False)
    places = jnp.arange(number_of)

    def named(sizes, turn):
        used = int((sizes > 0).sum())
        fixed = max(1, used // 4)
        moved = fixed + (places - fixed + turn * (used - fixed)) % max(1, number_of - fixed)
        return jnp.zeros((number_of,), jnp.int32).at[order[jnp.where(places < fixed, places, moved)]].set(jnp.asarray(sizes, jnp.int32))

    sizes = jnp.where(number % 4 == 0, named(packed, number // 4), named(usual, number - number // 4 - 1))
    mixed = jax.random.permutation(jax.random.fold_in(own, 3), number_of)
    donor, sink = mixed[0:number_of // 2 * 2:2], mixed[1:number_of // 2 * 2:2]
    margin = jnp.minimum(sizes[donor] - 1, most - sizes[sink]) // 2
    margin = jnp.where((donor == order[0]) | (sink == order[0]) | (sizes[sink] == 0), 0, jnp.maximum(margin, 0))
    moved = jax.random.randint(jax.random.fold_in(own, 4), (number_of // 2,), 0, 1 << 20) % (margin + 1)
    sizes = sizes.at[donor].add(-moved).at[sink].add(moved)
    items = jnp.searchsorted(jnp.cumsum(sizes), jnp.arange(rows * top), side="right").astype(jnp.int32)
    table = items.reshape(top, rows).T
    table = table[jax.random.permutation(jax.random.fold_in(own, 1), rows)]
    turn = jax.random.randint(jax.random.fold_in(own, 2), (rows, 1), 0, top)
    return jnp.take_along_axis(table, (jnp.arange(top)[None, :] + turn) % top, axis=1)


def shares(amount, total, most, lean, full):
    loads = [(1 << 20) // math.isqrt(standing ** lean) + 1 for standing in range(1, amount + 1)]
    largest = most if full else min(most, max(-(-total // amount), total * loads[0] // sum(loads)))
    least = 1 if total - largest >= amount - 1 else 0
    counts, rest = [largest] + [least] * (amount - 1), total - largest - least * (amount - 1)
    while rest > 0:
        movable = [i for i in range(1, amount) if counts[i] < largest] or [i for i in range(1, amount) if counts[i] < most]
        mass, remaining = sum([loads[i] for i in movable]), rest
        for i in movable:
            addition = min(most - counts[i], max(1, remaining * loads[i] // mass), rest)
            counts[i] = counts[i] + addition
            rest = rest - addition
    return np.array(counts)


def bell_draw(key, dims, scale, limit, shards=(), kind=jnp.bfloat16):
    gain = block_levels(key, dims, shards, -0.22, 0.18) if shards else 1.0
    entries = jax.random.normal(key, dims, jnp.float32) * scale * gain
    return jnp.minimum(jnp.maximum(entries, -limit), limit).astype(kind)


def setup_inputs(seed: int = 0) -> dict:
    splits = jax.random.split(jax.random.key(seed), 6)
    cotangent = bell_draw(splits[0], (TOKENS, D), 1.0, 6.0, ((0, 1024),))
    probs = jnp.clip(0.1 + 0.9 * jax.random.uniform(splits[1], (TOKENS, TOP), jnp.float32) ** block_levels(splits[1], (TOKENS, TOP), ((0, 1024),), -0.2, 0.2), 0.1, 1.0)
    expert_ids_keys = jax.random.split(jax.random.fold_in(splits[2], 1), TOKENS // GROUP)
    expert_ids_turns = jax.random.permutation(jax.random.fold_in(splits[2], 3), TOKENS // GROUP)
    expert_ids = jax.vmap(lambda own, number: deal_out(jax.random.fold_in(splits[2], 2), own, number, GROUP, EXPERTS, TOP, CAP, 2))(expert_ids_keys, expert_ids_turns).reshape((TOKENS, TOP))
    saved_hidden = bell_draw(splits[3], (N_DP * N_EXPERT * CAP, EXPERTS * FF), 0.05, 0.29882812, ((0, 8), (1, 128)))
    down_weight = bell_draw(splits[4], (D, EXPERTS * FF), D ** -0.5, 0.09375, ((1, 128),))
    return dict(cotangent=cotangent, probs=probs, expert_ids=expert_ids, saved_hidden=saved_hidden, down_weight=down_weight)


def slot_table(flat_ids):
    expert_range = jnp.arange(EXPERTS, dtype=jnp.int32)
    onehot = (flat_ids[:, :, None] == expert_range[None, None, :]).astype(jnp.int32)
    earlier = jnp.cumsum(onehot, axis=1) - onehot
    return jnp.sum(earlier * onehot, axis=2).astype(jnp.int32)


def reference(cotangent, probs, expert_ids, saved_hidden, down_weight):
    groups = N_DP * N_EXPERT
    scaled = (probs[:, :, None] * cotangent.astype(jnp.float32)[:, None, :]).astype(jnp.bfloat16)
    scaled_flat = scaled.reshape(groups, 2 * GROUP, D).astype(jnp.float32)
    flat_ids = expert_ids.reshape(groups, 2 * GROUP)
    slot_ids = slot_table(flat_ids)
    hidden = saved_hidden.reshape(N_DP, N_EXPERT * CAP, EXPERTS, FF)
    weight = down_weight.reshape(D, EXPERTS, FF)
    cap_range = jnp.arange(CAP, dtype=jnp.int32)

    def one_expert(expert_index):
        selector = ((flat_ids == expert_index)[:, None, :] & (slot_ids[:, None, :] == cap_range[None, :, None])).astype(jnp.float32)
        slot_rows = jnp.einsum("gsa,gad->gsd", selector, scaled_flat, precision=lax.Precision.HIGHEST).astype(jnp.bfloat16)
        slot_rows = slot_rows.reshape(N_DP, N_EXPERT * CAP, D)
        weight_cols = lax.dynamic_index_in_dim(weight, expert_index, 1, keepdims=False)
        hidden_cols = lax.dynamic_index_in_dim(hidden, expert_index, 2, keepdims=False)
        product = jnp.einsum("psd,df->psf", slot_rows.astype(jnp.float32), weight_cols.astype(jnp.float32))
        partial_value = jnp.sum(hidden_cols.astype(jnp.float32) * product, axis=2)

        def add_term(running, term_pair):
            rows_here, hidden_here = term_pair
            term = jnp.dot(rows_here.T, hidden_here, preferred_element_type=jnp.float32).astype(jnp.bfloat16)
            term = lax.optimization_barrier(term)
            return running + term.astype(jnp.float32), None

        summed, _ = lax.scan(add_term, jnp.zeros((D, FF), jnp.float32), (slot_rows, hidden_cols))
        return product.astype(jnp.bfloat16), summed.astype(jnp.bfloat16), partial_value

    grads, weight_parts, partials = lax.map(one_expert, jnp.arange(EXPERTS, dtype=jnp.int32))
    hidden_grad = grads.transpose(1, 2, 0, 3).reshape(N_DP * N_EXPERT * CAP, EXPERTS * FF)
    weight_grad = weight_parts.transpose(1, 0, 2).reshape(D, EXPERTS * FF)
    lookup = partials.reshape(EXPERTS, N_DP, N_EXPERT, CAP).transpose(1, 2, 0, 3).reshape(groups, EXPERTS, CAP)
    matches = (flat_ids[:, :, None] == jnp.arange(EXPERTS, dtype=jnp.int32)[None, None, :]).astype(jnp.float32)
    chosen = jnp.einsum("gae,ges->gas", matches, lookup, precision=lax.Precision.HIGHEST)
    values = jnp.sum(chosen * (slot_ids[:, :, None] == cap_range[None, None, :]).astype(jnp.float32), axis=2)
    prob_grad = values.reshape(TOKENS, TOP) / probs
    return hidden_grad, weight_grad, prob_grad
```

```python
import functools

import jax
import jax.numpy as jnp
from jax import lax
from jax.experimental import pallas as pl
from jax.experimental.pallas import tpu as pltpu
from jax.sharding import Mesh, PartitionSpec as P

PAD = 16
LANES = 128


def split3(value):
    high = value.astype(jnp.bfloat16)
    rest = value - high.astype(jnp.float32)
    middle = rest.astype(jnp.bfloat16)
    low = (rest - middle.astype(jnp.float32)).astype(jnp.bfloat16)
    return high, middle, low


def pack_kernel(cot_ref, probs_ref, out_ref):
    own_tokens = cot_ref.shape[0]
    place = lax.axis_index("tensor") * PAD
    lane = lax.broadcasted_iota(jnp.int32, (own_tokens, LANES), 1)
    token = lax.broadcasted_iota(jnp.int32, (own_tokens, LANES), 0)
    here = lane == token + place
    probs = probs_ref[...]
    out_ref[:own_tokens, :] = cot_ref[...]
    out_ref[own_tokens:, :] = jnp.zeros((PAD - own_tokens, cot_ref.shape[1]), jnp.bfloat16)
    rows = []
    for k in range(2):
        spread = jnp.sum(jnp.where(here, probs[:, k : k + 1], 0.0), axis=0, keepdims=True)
        rows.append(jnp.concatenate(split3(spread), axis=1))
    out_ref[own_tokens:, : 3 * LANES] = jnp.concatenate(rows, axis=0)


def fill_kernel(own_tokens, experts, capacity, gathered_ref, ids_ref, out_ref):
    members = gathered_ref.shape[0]
    group = members * own_tokens
    span = members * PAD
    lane = lax.broadcasted_iota(jnp.int32, (group, LANES), 1)
    token = lax.broadcasted_iota(jnp.int32, (group, LANES), 0)
    here = lane == token + (PAD - own_tokens) * (token // own_tokens)
    ids = ids_ref[...]
    lane_row = lax.broadcasted_iota(jnp.int32, (1, LANES), 1)
    real = (lane_row < span) & (lane_row % PAD < own_tokens)
    spread = [
        jnp.where(
            real, jnp.sum(jnp.where(here, ids[:, k : k + 1], 0), axis=0, keepdims=True), -1
        )
        for k in range(2)
    ]
    expert = lax.broadcasted_iota(jnp.int32, (experts, LANES), 0)
    named = [(spread[k] == expert).astype(jnp.float32) for k in range(2)]
    earlier_lane = lax.broadcasted_iota(jnp.int32, (LANES, LANES), 0)
    later_lane = lax.broadcasted_iota(jnp.int32, (LANES, LANES), 1)
    before = (earlier_lane < later_lane).astype(jnp.bfloat16)
    earlier = jnp.dot(
        (named[0] + named[1]).astype(jnp.bfloat16), before, preferred_element_type=jnp.float32
    )
    row = lax.broadcasted_iota(jnp.int32, (experts * capacity, LANES), 0)
    selector = jnp.zeros((experts * capacity, LANES), jnp.float32)
    weight = jnp.zeros((experts * capacity, LANES), jnp.float32)
    for k in range(2):
        count = earlier if k == 0 else earlier + named[0]
        slot = jnp.sum(count * named[k], axis=0, keepdims=True).astype(jnp.int32)
        key = jnp.where(spread[k] >= 0, spread[k] * capacity + slot, -1)
        parts = gathered_ref[:, own_tokens + k : own_tokens + k + 1, : 3 * LANES]
        parts = jnp.sum(parts.astype(jnp.float32), axis=0)
        prob = parts[:, :LANES] + parts[:, LANES : 2 * LANES] + parts[:, 2 * LANES :]
        match = row == key
        selector = jnp.where(match, 1.0, selector)
        weight = jnp.where(match, prob, weight)
    scale = jnp.sum(weight, axis=1, keepdims=True)
    picked = selector[:, :span].astype(jnp.bfloat16)
    step = 512
    for start in range(0, gathered_ref.shape[2], step):
        block = gathered_ref[:, :, start : start + step].reshape(span, step)
        rows = jnp.dot(picked, block, preferred_element_type=jnp.float32)
        out_ref[:, start : start + step] = (rows * scale).astype(jnp.bfloat16)


def assign_slots(flat_ids, experts):
    expert_range = jnp.arange(experts, dtype=jnp.int32)
    onehot = (flat_ids[:, None] == expert_range[None, :]).astype(jnp.int32)
    earlier = jnp.cumsum(onehot, axis=0) - onehot
    return jnp.sum(earlier * onehot, axis=1)


def shards(cotangent, probs, expert_ids, saved_hidden, down_weight):
    n_y, n_q, n_par = lax.axis_size("y"), lax.axis_size("zq"), lax.axis_size("par")
    members = lax.axis_size("tensor")
    n_expert = n_y * n_q * n_par
    experts = n_y * n_q
    own_tokens, model_width = cotangent.shape
    hidden_cols = saved_hidden.shape[1]
    capacity = saved_hidden.shape[0] // n_expert

    packed = pl.pallas_call(
        pack_kernel,
        out_shape=jax.ShapeDtypeStruct((PAD, model_width), jnp.bfloat16),
        compiler_params=pltpu.CompilerParams(vmem_limit_bytes=8 << 20),
    )(cotangent, probs)
    gathered = lax.all_gather(packed, "tensor", axis=0)
    buffer = pl.pallas_call(
        functools.partial(fill_kernel, own_tokens, experts, capacity),
        out_shape=jax.ShapeDtypeStruct((experts * capacity, model_width), jnp.bfloat16),
        compiler_params=pltpu.CompilerParams(vmem_limit_bytes=24 << 20),
    )(gathered, expert_ids)
    buffer = buffer.reshape(experts, capacity, model_width)
    own = lax.all_to_all(buffer, ("y", "zq"), split_axis=0, concat_axis=0, tiled=True)
    other = lax.ppermute(own, "par", [(0, 1), (1, 0)])
    is_even = lax.axis_index("par") == 0
    even = jnp.where(is_even, own, other)
    odd = jnp.where(is_even, other, own)
    rows = jnp.stack([even, odd], axis=1).reshape(n_expert * capacity, model_width)

    weight_grad = lax.psum_scatter(
        lax.dot_general(
            rows, saved_hidden, (((0,), (0,)), ((), ())), preferred_element_type=jnp.float32
        ).astype(jnp.bfloat16),
        "dp",
        scatter_dimension=0,
        tiled=True,
    )
    product = jnp.dot(rows, down_weight, preferred_element_type=jnp.float32)
    hidden_grad = product.astype(jnp.bfloat16)
    partial_value = jnp.sum(saved_hidden.astype(jnp.float32) * product, axis=1).reshape(
        n_expert, capacity
    )
    returned = lax.all_to_all(
        partial_value, ("y", "zq", "par"), split_axis=0, concat_axis=0, tiled=True
    )
    summed = lax.psum(returned, "tensor")
    lookup = jnp.sum(summed.reshape(experts, n_par, capacity), axis=1)
    flat_ids = expert_ids.reshape(-1)
    slot_ids = assign_slots(flat_ids, experts)
    start_row = lax.axis_index("tensor") * (own_tokens * 2)
    own_ids = lax.dynamic_slice_in_dim(flat_ids, start_row, own_tokens * 2)
    own_slots = lax.dynamic_slice_in_dim(slot_ids, start_row, own_tokens * 2)
    matches = (own_ids[:, None] == jnp.arange(experts, dtype=jnp.int32)[None, :]).astype(
        jnp.float32
    )
    chosen = jnp.dot(matches, lookup, precision=lax.Precision.HIGHEST)
    slot_match = (own_slots[:, None] == jnp.arange(capacity, dtype=jnp.int32)[None, :]).astype(
        jnp.float32
    )
    values = jnp.sum(chosen * slot_match, axis=1).reshape(own_tokens, 2)
    prob_grad = values / probs
    return (hidden_grad, weight_grad, prob_grad)


def solution(mesh):
    n_dp, n_expert, n_tensor = mesh.devices.shape
    fine = Mesh(
        mesh.devices.reshape(n_dp, 4, n_expert // 8, 2, n_tensor), ("dp", "y", "zq", "par", "tensor")
    )
    expert = ("y", "zq", "par")
    in_specs = (
        P(("dp",) + expert + ("tensor",), None),
        P(("dp",) + expert + ("tensor",), None),
        P(("dp",) + expert, None),
        P("dp", expert + ("tensor",)),
        P(None, expert + ("tensor",)),
    )
    out_specs = (
        P("dp", expert + ("tensor",)),
        P("dp", expert + ("tensor",)),
        P(("dp",) + expert + ("tensor",), None),
    )
    return jax.shard_map(shards, mesh=fine, in_specs=in_specs, out_specs=out_specs, check_vma=False)
```

```python
import functools

import jax
import jax.numpy as jnp
from jax import lax
from jax.experimental import pallas as pl
from jax.experimental.pallas import tpu as pltpu
from jax.sharding import Mesh, PartitionSpec as P

PAD = 16
LANES = 128


def split3(value):
    high = value.astype(jnp.bfloat16)
    rest = value - high.astype(jnp.float32)
    middle = rest.astype(jnp.bfloat16)
    low = (rest - middle.astype(jnp.float32)).astype(jnp.bfloat16)
    return high, middle, low


def pack_kernel(cot_ref, probs_ref, out_ref):
    own_tokens = cot_ref.shape[0]
    place = lax.axis_index("tensor") * PAD
    lane = lax.broadcasted_iota(jnp.int32, (own_tokens, LANES), 1)
    token = lax.broadcasted_iota(jnp.int32, (own_tokens, LANES), 0)
    here = lane == token + place
    probs = probs_ref[...]
    out_ref[:own_tokens, :] = cot_ref[...]
    out_ref[own_tokens:, :] = jnp.zeros((PAD - own_tokens, cot_ref.shape[1]), jnp.bfloat16)
    rows = []
    for k in range(2):
        spread = jnp.sum(jnp.where(here, probs[:, k : k + 1], 0.0), axis=0, keepdims=True)
        rows.append(jnp.concatenate(split3(spread), axis=1))
    out_ref[own_tokens:, : 3 * LANES] = jnp.concatenate(rows, axis=0)


def fill_kernel(own_tokens, experts, capacity, gathered_ref, ids_ref, out_ref):
    members = gathered_ref.shape[0]
    group = members * own_tokens
    span = members * PAD
    lane = lax.broadcasted_iota(jnp.int32, (group, LANES), 1)
    token = lax.broadcasted_iota(jnp.int32, (group, LANES), 0)
    here = lane == token + (PAD - own_tokens) * (token // own_tokens)
    ids = ids_ref[...]
    lane_row = lax.broadcasted_iota(jnp.int32, (1, LANES), 1)
    real = (lane_row < span) & (lane_row % PAD < own_tokens)
    spread = [
        jnp.where(
            real, jnp.sum(jnp.where(here, ids[:, k : k + 1], 0), axis=0, keepdims=True), -1
        )
        for k in range(2)
    ]
    expert = lax.broadcasted_iota(jnp.int32, (experts, LANES), 0)
    named = [(spread[k] == expert).astype(jnp.float32) for k in range(2)]
    earlier_lane = lax.broadcasted_iota(jnp.int32, (LANES, LANES), 0)
    later_lane = lax.broadcasted_iota(jnp.int32, (LANES, LANES), 1)
    before = (earlier_lane < later_lane).astype(jnp.bfloat16)
    earlier = jnp.dot(
        (named[0] + named[1]).astype(jnp.bfloat16), before, preferred_element_type=jnp.float32
    )
    row = lax.broadcasted_iota(jnp.int32, (experts * capacity, LANES), 0)
    selector = jnp.zeros((experts * capacity, LANES), jnp.float32)
    weight = jnp.zeros((experts * capacity, LANES), jnp.float32)
    for k in range(2):
        count = earlier if k == 0 else earlier + named[0]
        slot = jnp.sum(count * named[k], axis=0, keepdims=True).astype(jnp.int32)
        key = jnp.where(spread[k] >= 0, spread[k] * capacity + slot, -1)
        parts = gathered_ref[:, own_tokens + k : own_tokens + k + 1, : 3 * LANES]
        parts = jnp.sum(parts.astype(jnp.float32), axis=0)
        prob = parts[:, :LANES] + parts[:, LANES : 2 * LANES] + parts[:, 2 * LANES :]
        match = row == key
        selector = jnp.where(match, 1.0, selector)
        weight = jnp.where(match, prob, weight)
    scale = jnp.sum(weight, axis=1, keepdims=True)
    picked = selector[:, :span].astype(jnp.bfloat16)
    step = 512
    for start in range(0, gathered_ref.shape[2], step):
        block = gathered_ref[:, :, start : start + step].reshape(span, step)
        rows = jnp.dot(picked, block, preferred_element_type=jnp.float32)
        out_ref[:, start : start + step] = (rows * scale).astype(jnp.bfloat16)


def assign_slots(flat_ids, experts):
    expert_range = jnp.arange(experts, dtype=jnp.int32)
    onehot = (flat_ids[:, None] == expert_range[None, :]).astype(jnp.int32)
    earlier = jnp.cumsum(onehot, axis=0) - onehot
    return jnp.sum(earlier * onehot, axis=1)


def windows(n_dp, n_y, n_q, n_par, n_tensor):
    groups = []
    for dp in range(n_dp):
        for par in range(n_par):
            for run in range(n_tensor):
                group = []
                for y in range(n_y):
                    for q in range(n_q):
                        wraps = dp % 2 == 1 and q < n_q // 2
                        at = (run + 1) % n_tensor if wraps else run
                        group.append((((dp * n_y + y) * n_q + q) * n_par + par) * n_tensor + at)
                groups.append(group)
    return groups


def shards(cotangent, probs, expert_ids, saved_hidden, down_weight):
    n_y, n_q, n_par = lax.axis_size("y"), lax.axis_size("zq"), lax.axis_size("par")
    members = lax.axis_size("tensor")
    n_expert = n_y * n_q * n_par
    experts = n_y * n_q
    own_tokens, model_width = cotangent.shape
    hidden_cols = saved_hidden.shape[1]
    capacity = saved_hidden.shape[0] // n_expert

    packed = pl.pallas_call(
        pack_kernel,
        out_shape=jax.ShapeDtypeStruct((PAD, model_width), jnp.bfloat16),
        compiler_params=pltpu.CompilerParams(vmem_limit_bytes=8 << 20),
    )(cotangent, probs)
    gathered = lax.all_gather(packed, "tensor", axis=0)
    buffer = pl.pallas_call(
        functools.partial(fill_kernel, own_tokens, experts, capacity),
        out_shape=jax.ShapeDtypeStruct((experts * capacity, model_width), jnp.bfloat16),
        compiler_params=pltpu.CompilerParams(vmem_limit_bytes=24 << 20),
    )(gathered, expert_ids)
    buffer = buffer.reshape(experts, capacity, model_width)
    own = lax.all_to_all(
        buffer,
        ("dp", "y", "zq", "par", "tensor"),
        split_axis=0,
        concat_axis=0,
        axis_index_groups=windows(lax.axis_size("dp"), n_y, n_q, n_par, members),
        tiled=True,
    )
    other = lax.ppermute(own, "par", [(0, 1), (1, 0)])
    flat_ids = expert_ids.reshape(-1)
    keys = flat_ids * capacity + assign_slots(flat_ids, experts)
    start_row = lax.axis_index("tensor") * (own_tokens * 2)
    own_keys = lax.dynamic_slice_in_dim(keys, start_row, own_tokens * 2)
    own, other, own_keys = lax.optimization_barrier((own, other, own_keys))
    is_even = lax.axis_index("par") == 0
    even = jnp.where(is_even, own, other)
    odd = jnp.where(is_even, other, own)
    rows = jnp.stack([even, odd], axis=1).reshape(n_expert * capacity, model_width)

    weight_grad = lax.psum_scatter(
        lax.dot_general(
            rows, saved_hidden, (((0,), (0,)), ((), ())), preferred_element_type=jnp.float32
        ).astype(jnp.bfloat16),
        "dp",
        scatter_dimension=0,
        tiled=True,
    )
    product = jnp.dot(rows, down_weight, preferred_element_type=jnp.float32)
    hidden_grad = product.astype(jnp.bfloat16)
    partial_value = jnp.sum(saved_hidden.astype(jnp.float32) * product, axis=1).reshape(
        n_expert, capacity
    )
    returned = lax.all_to_all(
        partial_value, ("y", "zq", "par"), split_axis=0, concat_axis=0, tiled=True
    )
    returned = jnp.sum(returned.reshape(experts, n_par, capacity), axis=1)
    lookup = lax.psum(returned, "tensor").reshape(1, experts * capacity)
    chosen = own_keys[:, None] == jnp.arange(experts * capacity, dtype=jnp.int32)[None, :]
    values = jnp.sum(jnp.where(chosen, lookup, 0.0), axis=1).reshape(own_tokens, 2)
    prob_grad = values / probs
    return (hidden_grad, weight_grad, prob_grad)


def solution(mesh):
    n_dp, n_expert, n_tensor = mesh.devices.shape
    fine = Mesh(
        mesh.devices.reshape(n_dp, 4, n_expert // 8, 2, n_tensor), ("dp", "y", "zq", "par", "tensor")
    )
    expert = ("y", "zq", "par")
    in_specs = (
        P(("dp",) + expert + ("tensor",), None),
        P(("dp",) + expert + ("tensor",), None),
        P(("dp",) + expert, None),
        P("dp", expert + ("tensor",)),
        P(None, expert + ("tensor",)),
    )
    out_specs = (
        P("dp", expert + ("tensor",)),
        P("dp", expert + ("tensor",)),
        P(("dp",) + expert + ("tensor",), None),
    )
    return jax.shard_map(shards, mesh=fine, in_specs=in_specs, out_specs=out_specs, check_vma=False)
```

```python
import functools

import jax
import jax.numpy as jnp
from jax import lax
from jax.experimental import pallas as pl
from jax.experimental.pallas import tpu as pltpu
from jax.sharding import Mesh, PartitionSpec as P

PAD = 16
LANES = 128


def split3(value):
    high = value.astype(jnp.bfloat16)
    rest = value - high.astype(jnp.float32)
    middle = rest.astype(jnp.bfloat16)
    low = (rest - middle.astype(jnp.float32)).astype(jnp.bfloat16)
    return high, middle, low


def pack_kernel(cot_ref, probs_ref, out_ref):
    own_tokens = cot_ref.shape[0]
    place = lax.axis_index("tensor") * PAD
    lane = lax.broadcasted_iota(jnp.int32, (own_tokens, LANES), 1)
    token = lax.broadcasted_iota(jnp.int32, (own_tokens, LANES), 0)
    here = lane == token + place
    probs = probs_ref[...]
    out_ref[:own_tokens, :] = cot_ref[...]
    out_ref[own_tokens:, :] = jnp.zeros((PAD - own_tokens, cot_ref.shape[1]), jnp.bfloat16)
    rows = []
    for k in range(2):
        spread = jnp.sum(jnp.where(here, probs[:, k : k + 1], 0.0), axis=0, keepdims=True)
        rows.append(jnp.concatenate(split3(spread), axis=1))
    out_ref[own_tokens:, : 3 * LANES] = jnp.concatenate(rows, axis=0)


def fill_kernel(own_tokens, experts, capacity, gathered_ref, ids_ref, out_ref):
    members = gathered_ref.shape[0]
    group = members * own_tokens
    span = members * PAD
    lane = lax.broadcasted_iota(jnp.int32, (group, LANES), 1)
    token = lax.broadcasted_iota(jnp.int32, (group, LANES), 0)
    here = lane == token + (PAD - own_tokens) * (token // own_tokens)
    ids = ids_ref[...]
    lane_row = lax.broadcasted_iota(jnp.int32, (1, LANES), 1)
    real = (lane_row < span) & (lane_row % PAD < own_tokens)
    spread = [
        jnp.where(
            real, jnp.sum(jnp.where(here, ids[:, k : k + 1], 0), axis=0, keepdims=True), -1
        )
        for k in range(2)
    ]
    expert = lax.broadcasted_iota(jnp.int32, (experts, LANES), 0)
    named = [(spread[k] == expert).astype(jnp.float32) for k in range(2)]
    earlier_lane = lax.broadcasted_iota(jnp.int32, (LANES, LANES), 0)
    later_lane = lax.broadcasted_iota(jnp.int32, (LANES, LANES), 1)
    before = (earlier_lane < later_lane).astype(jnp.bfloat16)
    earlier = jnp.dot(
        (named[0] + named[1]).astype(jnp.bfloat16), before, preferred_element_type=jnp.float32
    )
    row = lax.broadcasted_iota(jnp.int32, (experts * capacity, LANES), 0)
    selector = jnp.zeros((experts * capacity, LANES), jnp.float32)
    weight = jnp.zeros((experts * capacity, LANES), jnp.float32)
    for k in range(2):
        count = earlier if k == 0 else earlier + named[0]
        slot = jnp.sum(count * named[k], axis=0, keepdims=True).astype(jnp.int32)
        key = jnp.where(spread[k] >= 0, spread[k] * capacity + slot, -1)
        parts = gathered_ref[:, own_tokens + k : own_tokens + k + 1, : 3 * LANES]
        parts = jnp.sum(parts.astype(jnp.float32), axis=0)
        prob = parts[:, :LANES] + parts[:, LANES : 2 * LANES] + parts[:, 2 * LANES :]
        match = row == key
        selector = jnp.where(match, 1.0, selector)
        weight = jnp.where(match, prob, weight)
    scale = jnp.sum(weight, axis=1, keepdims=True)
    picked = selector[:, :span].astype(jnp.bfloat16)
    step = 512
    for start in range(0, gathered_ref.shape[2], step):
        block = gathered_ref[:, :, start : start + step].reshape(span, step)
        rows = jnp.dot(picked, block, preferred_element_type=jnp.float32)
        out_ref[:, start : start + step] = (rows * scale).astype(jnp.bfloat16)


def assign_slots(flat_ids, experts):
    expert_range = jnp.arange(experts, dtype=jnp.int32)
    onehot = (flat_ids[:, None] == expert_range[None, :]).astype(jnp.int32)
    earlier = jnp.cumsum(onehot, axis=0) - onehot
    return jnp.sum(earlier * onehot, axis=1)


def windows(n_dp, n_y, n_q, n_par, n_tensor):
    groups = []
    for dp in range(n_dp):
        for par in range(n_par):
            for run in range(n_tensor):
                group = []
                for y in range(n_y):
                    for q in range(n_q):
                        wraps = dp % 2 == 1 and q < n_q // 2
                        at = (run + 1) % n_tensor if wraps else run
                        group.append((((dp * n_y + y) * n_q + q) * n_par + par) * n_tensor + at)
                groups.append(group)
    return groups


def shards(cotangent, probs, expert_ids, saved_hidden, down_weight):
    n_y, n_q, n_par = lax.axis_size("y"), lax.axis_size("zq"), lax.axis_size("par")
    members = lax.axis_size("tensor")
    n_expert = n_y * n_q * n_par
    experts = n_y * n_q
    own_tokens, model_width = cotangent.shape
    hidden_cols = saved_hidden.shape[1]
    capacity = saved_hidden.shape[0] // n_expert

    n_dp = lax.axis_size("dp")
    swap = [(0, 1), (1, 0)]
    is_even = lax.axis_index("par") == 0

    hidden = saved_hidden.reshape(experts, n_par, capacity, hidden_cols)
    hidden_mine = jnp.where(is_even, hidden[:, 0], hidden[:, 1])
    hidden_mine = hidden_mine.reshape(experts * capacity, hidden_cols)
    hidden_send = jnp.where(is_even, hidden[:, 1], hidden[:, 0])
    hidden_send = hidden_send.reshape(experts * capacity, hidden_cols)
    hidden_theirs = lax.ppermute(hidden_send, "par", swap)
    hidden_all = lax.all_gather(jnp.stack([hidden_mine, hidden_theirs]), "dp", axis=0)
    chunk = model_width // n_dp
    weight_send = lax.dynamic_slice_in_dim(down_weight, lax.axis_index("dp") * chunk, chunk)
    weight_theirs = lax.all_gather(
        lax.ppermute(weight_send, "par", swap), "dp", axis=0, tiled=True
    )

    packed = pl.pallas_call(
        pack_kernel,
        out_shape=jax.ShapeDtypeStruct((PAD, model_width), jnp.bfloat16),
        compiler_params=pltpu.CompilerParams(vmem_limit_bytes=8 << 20),
    )(cotangent, probs)
    gathered = lax.all_gather(packed, "tensor", axis=0)
    buffer = pl.pallas_call(
        functools.partial(fill_kernel, own_tokens, experts, capacity),
        out_shape=jax.ShapeDtypeStruct((experts * capacity, model_width), jnp.bfloat16),
        compiler_params=pltpu.CompilerParams(vmem_limit_bytes=24 << 20),
    )(gathered, expert_ids)
    buffer = buffer.reshape(experts, capacity, model_width)
    groups = windows(n_dp, n_y, n_q, n_par, members)
    every = ("dp", "y", "zq", "par", "tensor")
    rows = lax.all_to_all(
        buffer, every, split_axis=0, concat_axis=0, axis_index_groups=groups, tiled=True
    ).reshape(experts * capacity, model_width)

    flat_ids = expert_ids.reshape(-1)
    keys = flat_ids * capacity + assign_slots(flat_ids, experts)
    start_row = lax.axis_index("tensor") * (own_tokens * 2)
    own_keys = lax.dynamic_slice_in_dim(keys, start_row, own_tokens * 2)

    product = jnp.dot(rows, down_weight, preferred_element_type=jnp.float32)
    product_theirs = jnp.dot(rows, weight_theirs, preferred_element_type=jnp.float32)
    partial_value = jnp.sum(
        hidden_mine.astype(jnp.float32) * product
        + hidden_theirs.astype(jnp.float32) * product_theirs,
        axis=1,
    ).reshape(experts, capacity)
    swapped = lax.ppermute(product_theirs.astype(jnp.bfloat16), "par", swap)

    by_feature = rows.reshape(experts * capacity, n_dp, model_width // n_dp).transpose(1, 0, 2)
    replica_rows = lax.all_to_all(by_feature, "dp", split_axis=0, concat_axis=0, tiled=True)
    contract = (((0, 1), (0, 1)), ((), ()))
    term_theirs = lax.dot_general(
        replica_rows, hidden_all[:, 1], contract, preferred_element_type=jnp.float32
    ).astype(jnp.bfloat16)
    term_mine = lax.dot_general(
        replica_rows, hidden_all[:, 0], contract, preferred_element_type=jnp.float32
    )
    term_theirs, partial_value = lax.optimization_barrier((term_theirs, partial_value))
    term_swapped = lax.ppermute(term_theirs, "par", swap)
    weight_grad = (term_mine + term_swapped.astype(jnp.float32)).astype(jnp.bfloat16)

    mine = product.astype(jnp.bfloat16).reshape(experts, capacity, hidden_cols)
    swapped = swapped.reshape(experts, capacity, hidden_cols)
    even = jnp.where(is_even, mine, swapped)
    odd = jnp.where(is_even, swapped, mine)
    hidden_grad = jnp.stack([even, odd], axis=1).reshape(n_expert * capacity, hidden_cols)

    returned = lax.all_to_all(
        partial_value, every, split_axis=0, concat_axis=0, axis_index_groups=groups, tiled=True
    )
    lookup = lax.psum(returned, "tensor").reshape(1, experts * capacity)
    chosen = own_keys[:, None] == jnp.arange(experts * capacity, dtype=jnp.int32)[None, :]
    values = jnp.sum(jnp.where(chosen, lookup, 0.0), axis=1).reshape(own_tokens, 2)
    prob_grad = values / probs
    return (hidden_grad, weight_grad, prob_grad)


def solution(mesh):
    n_dp, n_expert, n_tensor = mesh.devices.shape
    fine = Mesh(
        mesh.devices.reshape(n_dp, 4, n_expert // 8, 2, n_tensor), ("dp", "y", "zq", "par", "tensor")
    )
    expert = ("y", "zq", "par")
    in_specs = (
        P(("dp",) + expert + ("tensor",), None),
        P(("dp",) + expert + ("tensor",), None),
        P(("dp",) + expert, None),
        P("dp", expert + ("tensor",)),
        P(None, expert + ("tensor",)),
    )
    out_specs = (
        P("dp", expert + ("tensor",)),
        P("dp", expert + ("tensor",)),
        P(("dp",) + expert + ("tensor",), None),
    )
    return jax.shard_map(shards, mesh=fine, in_specs=in_specs, out_specs=out_specs, check_vma=False)
```

```python
import functools

import jax
import jax.numpy as jnp
from jax import lax
from jax.experimental import pallas as pl
from jax.experimental.pallas import tpu as pltpu
from jax.sharding import Mesh, PartitionSpec as P

PAD = 16
LANES = 128


def split3(value):
    high = value.astype(jnp.bfloat16)
    rest = value - high.astype(jnp.float32)
    middle = rest.astype(jnp.bfloat16)
    low = (rest - middle.astype(jnp.float32)).astype(jnp.bfloat16)
    return high, middle, low


def pack_kernel(cot_ref, probs_ref, out_ref):
    own_tokens = cot_ref.shape[0]
    place = lax.axis_index("tensor") * PAD
    lane = lax.broadcasted_iota(jnp.int32, (own_tokens, LANES), 1)
    token = lax.broadcasted_iota(jnp.int32, (own_tokens, LANES), 0)
    here = lane == token + place
    probs = probs_ref[...]
    out_ref[:own_tokens, :] = cot_ref[...]
    out_ref[own_tokens:, :] = jnp.zeros((PAD - own_tokens, cot_ref.shape[1]), jnp.bfloat16)
    rows = []
    for k in range(2):
        spread = jnp.sum(jnp.where(here, probs[:, k : k + 1], 0.0), axis=0, keepdims=True)
        rows.append(jnp.concatenate(split3(spread), axis=1))
    out_ref[own_tokens:, : 3 * LANES] = jnp.concatenate(rows, axis=0)


def fill_kernel(own_tokens, experts, capacity, gathered_ref, ids_ref, out_ref):
    members = gathered_ref.shape[0]
    group = members * own_tokens
    span = members * PAD
    lane = lax.broadcasted_iota(jnp.int32, (group, LANES), 1)
    token = lax.broadcasted_iota(jnp.int32, (group, LANES), 0)
    here = lane == token + (PAD - own_tokens) * (token // own_tokens)
    ids = ids_ref[...]
    lane_row = lax.broadcasted_iota(jnp.int32, (1, LANES), 1)
    real = (lane_row < span) & (lane_row % PAD < own_tokens)
    spread = [
        jnp.where(
            real, jnp.sum(jnp.where(here, ids[:, k : k + 1], 0), axis=0, keepdims=True), -1
        )
        for k in range(2)
    ]
    expert = lax.broadcasted_iota(jnp.int32, (experts, LANES), 0)
    named = [(spread[k] == expert).astype(jnp.float32) for k in range(2)]
    earlier_lane = lax.broadcasted_iota(jnp.int32, (LANES, LANES), 0)
    later_lane = lax.broadcasted_iota(jnp.int32, (LANES, LANES), 1)
    before = (earlier_lane < later_lane).astype(jnp.bfloat16)
    earlier = jnp.dot(
        (named[0] + named[1]).astype(jnp.bfloat16), before, preferred_element_type=jnp.float32
    )
    row = lax.broadcasted_iota(jnp.int32, (experts * capacity, LANES), 0)
    selector = jnp.zeros((experts * capacity, LANES), jnp.float32)
    weight = jnp.zeros((experts * capacity, LANES), jnp.float32)
    for k in range(2):
        count = earlier if k == 0 else earlier + named[0]
        slot = jnp.sum(count * named[k], axis=0, keepdims=True).astype(jnp.int32)
        key = jnp.where(spread[k] >= 0, spread[k] * capacity + slot, -1)
        parts = gathered_ref[:, own_tokens + k : own_tokens + k + 1, : 3 * LANES]
        parts = jnp.sum(parts.astype(jnp.float32), axis=0)
        prob = parts[:, :LANES] + parts[:, LANES : 2 * LANES] + parts[:, 2 * LANES :]
        match = row == key
        selector = jnp.where(match, 1.0, selector)
        weight = jnp.where(match, prob, weight)
    scale = jnp.sum(weight, axis=1, keepdims=True)
    picked = selector[:, :span].astype(jnp.bfloat16)
    step = 512
    for start in range(0, gathered_ref.shape[2], step):
        block = gathered_ref[:, :, start : start + step].reshape(span, step)
        rows = jnp.dot(picked, block, preferred_element_type=jnp.float32)
        out_ref[:, start : start + step] = (rows * scale).astype(jnp.bfloat16)


def parity_order(rows, capacity, from_natural):
    lanes = rows // 2
    axes = (0, 1) if from_natural else (1, 0)
    natural = lax.broadcasted_iota(jnp.int32, (rows, rows), axes[0])
    ordered = lax.broadcasted_iota(jnp.int32, (rows, rows), axes[1])
    here = lax.axis_index("par")
    parity = jnp.where(ordered < lanes, here, 1 - here)
    within = ordered % lanes
    source = (within // capacity) * (2 * capacity) + parity * capacity + within % capacity
    return (natural == source).astype(jnp.bfloat16)


def sort_kernel(capacity, hidden_ref, mine_ref, send_ref):
    rows = hidden_ref.shape[1]
    order = parity_order(rows, capacity, True)
    moved = jnp.dot(hidden_ref[...], order, preferred_element_type=jnp.float32)
    moved = moved.astype(jnp.bfloat16)
    mine_ref[...] = moved[:, : rows // 2]
    send_ref[...] = moved[:, rows // 2 :]


def unsort_kernel(capacity, mine_ref, theirs_ref, out_ref):
    rows = out_ref.shape[1]
    order = parity_order(rows, capacity, False)
    both = jnp.concatenate([mine_ref[...], theirs_ref[...]], axis=1)
    out_ref[...] = jnp.dot(both, order, preferred_element_type=jnp.float32).astype(jnp.bfloat16)


def product_kernel(
    capacity,
    rows_ref,
    weight_ref,
    weight_theirs_ref,
    hidden_ref,
    hidden_theirs_ref,
    mine_ref,
    theirs_ref,
    partial_ref,
    by_feature_ref,
    total,
):
    step = pl.program_id(0)

    @pl.when(step == 0)
    def _():
        total[...] = jnp.zeros_like(total)

    rows = rows_ref[...]
    by_feature_ref[0] = rows
    contract = (((1,), (1,)), ((), ()))
    total[0] += lax.dot_general(
        weight_ref[...], rows, contract, preferred_element_type=jnp.float32
    )
    total[1] += lax.dot_general(
        weight_theirs_ref[0], rows, contract, preferred_element_type=jnp.float32
    )

    @pl.when(step == pl.num_programs(0) - 1)
    def _():
        mine, theirs = total[0], total[1]
        mine_ref[...] = mine.astype(jnp.bfloat16)
        theirs_ref[...] = theirs.astype(jnp.bfloat16)
        summed = jnp.sum(
            hidden_ref[...].astype(jnp.float32) * mine
            + hidden_theirs_ref[...].astype(jnp.float32) * theirs,
            axis=0,
            keepdims=True,
        )
        lanes = summed.shape[1]
        experts = partial_ref.shape[0]
        of_expert = lax.broadcasted_iota(jnp.int32, (experts, lanes), 1) // capacity
        expert = lax.broadcasted_iota(jnp.int32, (experts, lanes), 0)
        spread = jnp.where(of_expert == expert, summed, 0.0)
        at = lax.broadcasted_iota(jnp.int32, (lanes, LANES), 0) % capacity
        slot = lax.broadcasted_iota(jnp.int32, (lanes, LANES), 1)
        partial_ref[...] = jnp.dot(
            spread,
            (at == slot).astype(jnp.float32),
            precision=lax.Precision.HIGHEST,
            preferred_element_type=jnp.float32,
        )


def term_kernel(hidden_ref, rows_ref, mine_ref, theirs_ref, total):
    step = pl.program_id(0)

    @pl.when(step == 0)
    def _():
        total[...] = jnp.zeros_like(total)

    rows = rows_ref[0]
    for half in range(2):
        total[half] += jnp.dot(hidden_ref[0, half], rows, preferred_element_type=jnp.float32)

    @pl.when(step == pl.num_programs(0) - 1)
    def _():
        mine_ref[...] = total[0]
        theirs_ref[...] = total[1].astype(jnp.bfloat16)


def assign_slots(flat_ids, experts):
    expert_range = jnp.arange(experts, dtype=jnp.int32)
    onehot = (flat_ids[:, None] == expert_range[None, :]).astype(jnp.int32)
    earlier = jnp.cumsum(onehot, axis=0) - onehot
    return jnp.sum(earlier * onehot, axis=1)


def windows(n_dp, n_y, n_q, n_par, n_tensor):
    groups = []
    for dp in range(n_dp):
        for par in range(n_par):
            for run in range(n_tensor):
                group = []
                for y in range(n_y):
                    for q in range(n_q):
                        wraps = dp % 2 == 1 and q < n_q // 2
                        at = (run + 1) % n_tensor if wraps else run
                        group.append((((dp * n_y + y) * n_q + q) * n_par + par) * n_tensor + at)
                groups.append(group)
    return groups


def shards(cotangent, probs, expert_ids, saved_hidden, down_weight):
    n_y, n_q, n_par = lax.axis_size("y"), lax.axis_size("zq"), lax.axis_size("par")
    members = lax.axis_size("tensor")
    n_expert = n_y * n_q * n_par
    experts = n_y * n_q
    own_tokens, model_width = cotangent.shape
    hidden_cols = saved_hidden.shape[1]
    capacity = saved_hidden.shape[0] // n_expert

    n_dp = lax.axis_size("dp")
    chunk = model_width // n_dp
    half = experts * capacity
    swap = [(0, 1), (1, 0)]
    large = pltpu.CompilerParams(vmem_limit_bytes=56 << 20)
    small = pltpu.CompilerParams(vmem_limit_bytes=16 << 20)

    weight = down_weight.T
    weight_send = lax.dynamic_slice_in_dim(weight, lax.axis_index("dp") * chunk, chunk, axis=1)
    weight_swapped = lax.ppermute(weight_send, "par", swap)
    hidden_mine, hidden_send = pl.pallas_call(
        functools.partial(sort_kernel, capacity),
        out_shape=[jax.ShapeDtypeStruct((hidden_cols, half), jnp.bfloat16)] * 2,
        compiler_params=small,
    )(saved_hidden.T)
    hidden_theirs = lax.ppermute(hidden_send, "par", swap)
    packed = pl.pallas_call(
        pack_kernel,
        out_shape=jax.ShapeDtypeStruct((PAD, model_width), jnp.bfloat16),
        compiler_params=small,
    )(cotangent, probs)
    packed, weight_swapped, hidden_theirs = lax.optimization_barrier(
        (packed, weight_swapped, hidden_theirs)
    )
    weight_theirs = lax.all_gather(weight_swapped, "dp", axis=0)
    hidden_all = lax.all_gather(jnp.stack([hidden_mine, hidden_theirs]), "dp", axis=0)

    gathered = lax.all_gather(packed, "tensor", axis=0)
    buffer = pl.pallas_call(
        functools.partial(fill_kernel, own_tokens, experts, capacity),
        out_shape=jax.ShapeDtypeStruct((half, model_width), jnp.bfloat16),
        compiler_params=pltpu.CompilerParams(vmem_limit_bytes=24 << 20),
    )(gathered, expert_ids)
    buffer, weight_theirs = lax.optimization_barrier((buffer, weight_theirs))
    buffer = buffer.reshape(experts, capacity, model_width)
    groups = windows(n_dp, n_y, n_q, n_par, members)
    every = ("dp", "y", "zq", "par", "tensor")
    rows = lax.all_to_all(
        buffer, every, split_axis=0, concat_axis=0, axis_index_groups=groups, tiled=True
    ).reshape(half, model_width)

    flat_ids = expert_ids.reshape(-1)
    keys = flat_ids * capacity + assign_slots(flat_ids, experts)
    start_row = lax.axis_index("tensor") * (own_tokens * 2)
    own_keys = lax.dynamic_slice_in_dim(keys, start_row, own_tokens * 2)
    rows, own_keys = lax.optimization_barrier((rows, own_keys))

    whole = pl.BlockSpec((hidden_cols, half), lambda i: (0, 0))
    product, product_theirs, partial_value, by_feature = pl.pallas_call(
        functools.partial(product_kernel, capacity),
        grid=(n_dp,),
        in_specs=[
            pl.BlockSpec((half, chunk), lambda i: (0, i)),
            pl.BlockSpec((hidden_cols, chunk), lambda i: (0, i)),
            pl.BlockSpec((1, hidden_cols, chunk), lambda i: (i, 0, 0)),
            whole,
            whole,
        ],
        out_specs=[
            whole,
            whole,
            pl.BlockSpec((experts, LANES), lambda i: (0, 0)),
            pl.BlockSpec((1, half, chunk), lambda i: (i, 0, 0)),
        ],
        out_shape=[
            jax.ShapeDtypeStruct((hidden_cols, half), jnp.bfloat16),
            jax.ShapeDtypeStruct((hidden_cols, half), jnp.bfloat16),
            jax.ShapeDtypeStruct((experts, LANES), jnp.float32),
            jax.ShapeDtypeStruct((n_dp, half, chunk), jnp.bfloat16),
        ],
        scratch_shapes=[pltpu.VMEM((2, hidden_cols, half), jnp.float32)],
        compiler_params=large,
    )(rows, weight, weight_theirs, hidden_mine, hidden_theirs)

    replica_rows = lax.all_to_all(by_feature, "dp", split_axis=0, concat_axis=0, tiled=True)
    partial_value = lax.psum(partial_value, "tensor")
    product_swapped = lax.ppermute(product_theirs, "par", swap)
    square = pl.BlockSpec((hidden_cols, chunk), lambda i: (0, 0))
    term, term_theirs = pl.pallas_call(
        term_kernel,
        grid=(n_dp,),
        in_specs=[
            pl.BlockSpec((1, 2, hidden_cols, half), lambda i: (i, 0, 0, 0)),
            pl.BlockSpec((1, half, chunk), lambda i: (i, 0, 0)),
        ],
        out_specs=[square, square],
        out_shape=[
            jax.ShapeDtypeStruct((hidden_cols, chunk), jnp.float32),
            jax.ShapeDtypeStruct((hidden_cols, chunk), jnp.bfloat16),
        ],
        scratch_shapes=[pltpu.VMEM((2, hidden_cols, chunk), jnp.float32)],
        compiler_params=large,
    )(hidden_all, replica_rows)
    hidden_grad = pl.pallas_call(
        functools.partial(unsort_kernel, capacity),
        out_shape=jax.ShapeDtypeStruct((hidden_cols, 2 * half), jnp.bfloat16),
        compiler_params=small,
    )(product, product_swapped)
    partial_value, term_theirs = lax.optimization_barrier((partial_value, term_theirs))
    term_swapped = lax.ppermute(term_theirs, "par", swap)
    lookup = lax.all_to_all(
        partial_value, every, split_axis=0, concat_axis=0, axis_index_groups=groups, tiled=True
    )
    weight_grad = (term + term_swapped.astype(jnp.float32)).astype(jnp.bfloat16).T
    hidden_grad = hidden_grad.T

    expert = lax.broadcasted_iota(jnp.int32, (1, experts, LANES), 1)
    slot = lax.broadcasted_iota(jnp.int32, (1, experts, LANES), 2)
    chosen = (own_keys[:, None, None] == expert * capacity + slot) & (slot < capacity)
    values = jnp.sum(jnp.where(chosen, lookup[None], 0.0), axis=(1, 2)).reshape(own_tokens, 2)
    prob_grad = values / probs
    return (hidden_grad, weight_grad, prob_grad)


def solution(mesh):
    n_dp, n_expert, n_tensor = mesh.devices.shape
    fine = Mesh(
        mesh.devices.reshape(n_dp, 4, n_expert // 8, 2, n_tensor), ("dp", "y", "zq", "par", "tensor")
    )
    expert = ("y", "zq", "par")
    in_specs = (
        P(("dp",) + expert + ("tensor",), None),
        P(("dp",) + expert + ("tensor",), None),
        P(("dp",) + expert, None),
        P("dp", expert + ("tensor",)),
        P(None, expert + ("tensor",)),
    )
    out_specs = (
        P("dp", expert + ("tensor",)),
        P("dp", expert + ("tensor",)),
        P(("dp",) + expert + ("tensor",), None),
    )
    return jax.shard_map(shards, mesh=fine, in_specs=in_specs, out_specs=out_specs, check_vma=False)
```

```python
import functools

import jax
import jax.numpy as jnp
from jax import lax
from jax.experimental import pallas as pl
from jax.experimental.pallas import tpu as pltpu
from jax.sharding import Mesh, PartitionSpec as P

PAD = 16
LANES = 128


def split3(value):
    high = value.astype(jnp.bfloat16)
    rest = value - high.astype(jnp.float32)
    middle = rest.astype(jnp.bfloat16)
    low = (rest - middle.astype(jnp.float32)).astype(jnp.bfloat16)
    return high, middle, low


def pack_kernel(cot_ref, probs_ref, out_ref):
    own_tokens = cot_ref.shape[0]
    place = lax.axis_index("tensor") * PAD
    lane = lax.broadcasted_iota(jnp.int32, (own_tokens, LANES), 1)
    token = lax.broadcasted_iota(jnp.int32, (own_tokens, LANES), 0)
    here = (lane == token + place).astype(jnp.bfloat16)
    parts = [
        jnp.dot(part, here, preferred_element_type=jnp.float32).astype(jnp.bfloat16)
        for part in split3(probs_ref[...])
    ]
    out_ref[:own_tokens, :] = cot_ref[...]
    out_ref[own_tokens:, :] = jnp.zeros((PAD - own_tokens, cot_ref.shape[1]), jnp.bfloat16)
    out_ref[own_tokens:, : 3 * LANES] = jnp.concatenate(parts, axis=1)


def fill_kernel(own_tokens, experts, capacity, gathered_ref, ids_ref, out_ref):
    members = gathered_ref.shape[0]
    group = members * own_tokens
    span = members * PAD
    lane = lax.broadcasted_iota(jnp.int32, (group, LANES), 1)
    token = lax.broadcasted_iota(jnp.int32, (group, LANES), 0)
    here = lane == token + (PAD - own_tokens) * (token // own_tokens)
    moved = jnp.dot(
        ids_ref[...].astype(jnp.float32).astype(jnp.bfloat16),
        here.astype(jnp.bfloat16),
        preferred_element_type=jnp.float32,
    ).astype(jnp.int32)
    lane_row = lax.broadcasted_iota(jnp.int32, (1, LANES), 1)
    real = (lane_row < span) & (lane_row % PAD < own_tokens)
    spread = [jnp.where(real, moved[k : k + 1], -1) for k in range(2)]
    expert = lax.broadcasted_iota(jnp.int32, (experts, LANES), 0)
    named = [(spread[k] == expert).astype(jnp.float32) for k in range(2)]
    earlier_lane = lax.broadcasted_iota(jnp.int32, (LANES, LANES), 0)
    later_lane = lax.broadcasted_iota(jnp.int32, (LANES, LANES), 1)
    before = (earlier_lane < later_lane).astype(jnp.bfloat16)
    earlier = jnp.dot(
        (named[0] + named[1]).astype(jnp.bfloat16), before, preferred_element_type=jnp.float32
    )
    row = lax.broadcasted_iota(jnp.int32, (experts * capacity, LANES), 0)
    selector = jnp.zeros((experts * capacity, LANES), jnp.float32)
    weight = jnp.zeros((experts * capacity, LANES), jnp.float32)
    for k in range(2):
        count = earlier if k == 0 else earlier + named[0]
        slot = jnp.sum(count * named[k], axis=0, keepdims=True).astype(jnp.int32)
        key = jnp.where(spread[k] >= 0, spread[k] * capacity + slot, -1)
        parts = gathered_ref[:, own_tokens + k : own_tokens + k + 1, : 3 * LANES]
        parts = jnp.sum(parts.astype(jnp.float32), axis=0)
        prob = parts[:, :LANES] + parts[:, LANES : 2 * LANES] + parts[:, 2 * LANES :]
        match = row == key
        selector = jnp.where(match, 1.0, selector)
        weight = jnp.where(match, prob, weight)
    scale = jnp.sum(weight, axis=1, keepdims=True)
    picked = selector[:, :span].astype(jnp.bfloat16)
    step = 512
    for start in range(0, gathered_ref.shape[2], step):
        block = gathered_ref[:, :, start : start + step].reshape(span, step)
        rows = jnp.dot(picked, block, preferred_element_type=jnp.float32)
        out_ref[:, start : start + step] = (rows * scale).astype(jnp.bfloat16)


def parity_order(rows, capacity, from_natural):
    lanes = rows // 2
    axes = (0, 1) if from_natural else (1, 0)
    natural = lax.broadcasted_iota(jnp.int32, (rows, rows), axes[0])
    ordered = lax.broadcasted_iota(jnp.int32, (rows, rows), axes[1])
    here = lax.axis_index("par")
    parity = jnp.where(ordered < lanes, here, 1 - here)
    within = ordered % lanes
    source = (within // capacity) * (2 * capacity) + parity * capacity + within % capacity
    return (natural == source).astype(jnp.bfloat16)


def sort_kernel(capacity, hidden_ref, mine_ref, send_ref):
    rows = hidden_ref.shape[1]
    order = parity_order(rows, capacity, True)
    moved = jnp.dot(hidden_ref[...], order, preferred_element_type=jnp.float32)
    moved = moved.astype(jnp.bfloat16)
    mine_ref[...] = moved[:, : rows // 2]
    send_ref[...] = moved[:, rows // 2 :]


def product_kernel(
    capacity,
    rows_ref,
    weight_ref,
    weight_theirs_ref,
    hidden_ref,
    hidden_theirs_ref,
    mine_ref,
    theirs_ref,
    partial_ref,
    by_feature_ref,
    both,
    total,
    sems,
):
    replicas, cols, chunk = weight_theirs_ref.shape
    stages, _, width = both.shape
    per_stage = width // chunk
    copies = []
    for stage in range(stages):
        here = [
            pltpu.make_async_copy(
                weight_ref.at[:, stage * width : (stage + 1) * width],
                both.at[stage, :cols],
                sems.at[stage, 0],
            )
        ]
        for part in range(per_stage):
            here.append(
                pltpu.make_async_copy(
                    weight_theirs_ref.at[stage * per_stage + part],
                    both.at[stage, cols:, part * chunk : (part + 1) * chunk],
                    sems.at[stage, 1 + part],
                )
            )
        for copy in here:
            copy.start()
        copies.append(here)
    for index in range(replicas):
        by_feature_ref[index] = rows_ref[:, index * chunk : (index + 1) * chunk]
    contract = (((1,), (1,)), ((), ()))
    for stage in range(stages):
        for copy in copies[stage]:
            copy.wait()
        rows = rows_ref[:, stage * width : (stage + 1) * width]
        added = lax.dot_general(both[stage], rows, contract, preferred_element_type=jnp.float32)
        total[...] = added if stage == 0 else total[...] + added
    mine, theirs = total[:cols], total[cols:]
    mine_ref[...] = mine.astype(jnp.bfloat16)
    theirs_ref[...] = theirs.astype(jnp.bfloat16)
    summed = jnp.sum(
        hidden_ref[...].astype(jnp.float32) * mine
        + hidden_theirs_ref[...].astype(jnp.float32) * theirs,
        axis=0,
        keepdims=True,
    )
    lanes = summed.shape[1]
    experts = partial_ref.shape[0]
    of_expert = lax.broadcasted_iota(jnp.int32, (experts, lanes), 1) // capacity
    expert = lax.broadcasted_iota(jnp.int32, (experts, lanes), 0)
    spread = jnp.where(of_expert == expert, summed, 0.0)
    at = lax.broadcasted_iota(jnp.int32, (lanes, LANES), 0) % capacity
    slot = lax.broadcasted_iota(jnp.int32, (lanes, LANES), 1)
    partial_ref[...] = jnp.dot(
        spread,
        (at == slot).astype(jnp.float32),
        precision=lax.Precision.HIGHEST,
        preferred_element_type=jnp.float32,
    )


def term_of(hidden_ref, rows_ref, half):
    replicas, depth, chunk = rows_ref.shape
    rows = rows_ref[...].reshape(replicas * depth, chunk)
    hidden = jnp.concatenate([hidden_ref[p, half] for p in range(replicas)], axis=1)
    return jnp.dot(hidden, rows, preferred_element_type=jnp.float32)


def send_kernel(hidden_ref, rows_ref, product_ref, out_ref):
    chunk = rows_ref.shape[2]
    out_ref[:, :chunk] = term_of(hidden_ref, rows_ref, 1).astype(jnp.bfloat16)
    out_ref[:, chunk:] = product_ref[...]


def keep_kernel(hidden_ref, rows_ref, out_ref):
    out_ref[...] = term_of(hidden_ref, rows_ref, 0)


def finish_kernel(capacity, term_ref, product_ref, swapped_ref, weight_ref, hidden_ref):
    chunk = term_ref.shape[1]
    term = term_ref[...] + swapped_ref[:, :chunk].astype(jnp.float32)
    weight_ref[...] = term.astype(jnp.bfloat16)
    order = parity_order(hidden_ref.shape[1], capacity, False)
    both = jnp.concatenate([product_ref[...], swapped_ref[:, chunk:]], axis=1)
    moved = jnp.dot(both, order, preferred_element_type=jnp.float32)
    hidden_ref[...] = moved.astype(jnp.bfloat16)


def assign_slots(flat_ids, experts):
    expert_range = jnp.arange(experts, dtype=jnp.int32)
    onehot = (flat_ids[:, None] == expert_range[None, :]).astype(jnp.int32)
    earlier = jnp.cumsum(onehot, axis=0) - onehot
    return jnp.sum(earlier * onehot, axis=1)


def windows(n_dp, n_y, n_q, n_par, n_tensor):
    groups = []
    for dp in range(n_dp):
        for par in range(n_par):
            for run in range(n_tensor):
                group = []
                for y in range(n_y):
                    for q in range(n_q):
                        wraps = dp % 2 == 1 and q < n_q // 2
                        at = (run + 1) % n_tensor if wraps else run
                        group.append((((dp * n_y + y) * n_q + q) * n_par + par) * n_tensor + at)
                groups.append(group)
    return groups


def shards(cotangent, probs, expert_ids, saved_hidden, down_weight):
    n_y, n_q, n_par = lax.axis_size("y"), lax.axis_size("zq"), lax.axis_size("par")
    members = lax.axis_size("tensor")
    n_expert = n_y * n_q * n_par
    experts = n_y * n_q
    own_tokens, model_width = cotangent.shape
    hidden_cols = saved_hidden.shape[1]
    capacity = saved_hidden.shape[0] // n_expert

    n_dp = lax.axis_size("dp")
    chunk = model_width // n_dp
    half = experts * capacity
    swap = [(0, 1), (1, 0)]
    small = pltpu.CompilerParams(vmem_limit_bytes=16 << 20)

    weight = down_weight.T
    weight_send = lax.dynamic_slice_in_dim(weight, lax.axis_index("dp") * chunk, chunk, axis=1)
    weight_swapped = lax.ppermute(weight_send, "par", swap)
    hidden_mine, hidden_send = pl.pallas_call(
        functools.partial(sort_kernel, capacity),
        out_shape=[jax.ShapeDtypeStruct((hidden_cols, half), jnp.bfloat16)] * 2,
        compiler_params=small,
    )(saved_hidden.T)
    hidden_theirs = lax.ppermute(hidden_send, "par", swap)
    packed = pl.pallas_call(
        pack_kernel,
        out_shape=jax.ShapeDtypeStruct((PAD, model_width), jnp.bfloat16),
        compiler_params=small,
    )(cotangent, probs.T)
    packed, weight_swapped = lax.optimization_barrier((packed, weight_swapped))
    weight_theirs = lax.all_gather(weight_swapped, "dp", axis=0)
    hidden_all = lax.all_gather(jnp.stack([hidden_mine, hidden_theirs]), "dp", axis=0)

    gathered = lax.all_gather(packed, "tensor", axis=0)
    buffer = pl.pallas_call(
        functools.partial(fill_kernel, own_tokens, experts, capacity),
        out_shape=jax.ShapeDtypeStruct((half, model_width), jnp.bfloat16),
        compiler_params=pltpu.CompilerParams(vmem_limit_bytes=24 << 20),
    )(gathered, expert_ids.T)
    buffer, weight_theirs = lax.optimization_barrier((buffer, weight_theirs))
    buffer = buffer.reshape(experts, capacity, model_width)
    groups = windows(n_dp, n_y, n_q, n_par, members)
    every = ("dp", "y", "zq", "par", "tensor")
    rows = lax.all_to_all(
        buffer, every, split_axis=0, concat_axis=0, axis_index_groups=groups, tiled=True
    ).reshape(half, model_width)

    flat_ids = expert_ids.reshape(-1)
    keys = flat_ids * capacity + assign_slots(flat_ids, experts)
    start_row = lax.axis_index("tensor") * (own_tokens * 2)
    own_keys = lax.dynamic_slice_in_dim(keys, start_row, own_tokens * 2)
    rows, own_keys = lax.optimization_barrier((rows, own_keys))

    vmem = pl.BlockSpec(memory_space=pltpu.VMEM)
    hbm = pl.BlockSpec(memory_space=pltpu.HBM)
    stages = 4
    product, product_theirs, partial_value, by_feature = pl.pallas_call(
        functools.partial(product_kernel, capacity),
        in_specs=[vmem, hbm, hbm, vmem, vmem],
        out_specs=[vmem] * 4,
        out_shape=[
            jax.ShapeDtypeStruct((hidden_cols, half), jnp.bfloat16),
            jax.ShapeDtypeStruct((hidden_cols, half), jnp.bfloat16),
            jax.ShapeDtypeStruct((experts, LANES), jnp.float32),
            jax.ShapeDtypeStruct((n_dp, half, chunk), jnp.bfloat16),
        ],
        scratch_shapes=[
            pltpu.VMEM((stages, 2 * hidden_cols, model_width // stages), jnp.bfloat16),
            pltpu.VMEM((2 * hidden_cols, half), jnp.float32),
            pltpu.SemaphoreType.DMA((stages, 1 + n_dp // stages)),
        ],
        compiler_params=pltpu.CompilerParams(vmem_limit_bytes=50 << 20),
    )(rows, weight, weight_theirs, hidden_mine, hidden_theirs)

    replica_rows = lax.all_to_all(by_feature, "dp", split_axis=0, concat_axis=0, tiled=True)
    partial_value = lax.psum(partial_value, "tensor")
    partial_value, replica_rows = lax.optimization_barrier((partial_value, replica_rows))
    term_cost = pl.CostEstimate(
        flops=2 * n_dp * half * hidden_cols * chunk,
        bytes_accessed=2 * n_dp * half * (hidden_cols + chunk) + 4 * hidden_cols * chunk,
        transcendentals=0,
    )
    medium = pltpu.CompilerParams(vmem_limit_bytes=24 << 20)
    sent = pl.pallas_call(
        send_kernel,
        out_shape=jax.ShapeDtypeStruct((hidden_cols, chunk + half), jnp.bfloat16),
        cost_estimate=term_cost,
        compiler_params=medium,
    )(hidden_all, replica_rows, product_theirs)
    swapped = lax.ppermute(sent, "par", swap)
    term = pl.pallas_call(
        keep_kernel,
        out_shape=jax.ShapeDtypeStruct((hidden_cols, chunk), jnp.float32),
        cost_estimate=term_cost,
        compiler_params=medium,
    )(hidden_all, replica_rows)
    weight_grad, hidden_grad = pl.pallas_call(
        functools.partial(finish_kernel, capacity),
        out_shape=[
            jax.ShapeDtypeStruct((hidden_cols, chunk), jnp.bfloat16),
            jax.ShapeDtypeStruct((hidden_cols, 2 * half), jnp.bfloat16),
        ],
        compiler_params=medium,
    )(term, product, swapped)
    weight_grad, hidden_grad = weight_grad.T, hidden_grad.T
    lookup = lax.all_to_all(
        partial_value, every, split_axis=0, concat_axis=0, axis_index_groups=groups, tiled=True
    )

    expert = lax.broadcasted_iota(jnp.int32, (1, experts, LANES), 1)
    slot = lax.broadcasted_iota(jnp.int32, (1, experts, LANES), 2)
    chosen = (own_keys[:, None, None] == expert * capacity + slot) & (slot < capacity)
    values = jnp.sum(jnp.where(chosen, lookup[None], 0.0), axis=(1, 2)).reshape(own_tokens, 2)
    prob_grad = values / probs
    return (hidden_grad, weight_grad, prob_grad)


def solution(mesh):
    n_dp, n_expert, n_tensor = mesh.devices.shape
    fine = Mesh(
        mesh.devices.reshape(n_dp, 4, n_expert // 8, 2, n_tensor), ("dp", "y", "zq", "par", "tensor")
    )
    expert = ("y", "zq", "par")
    in_specs = (
        P(("dp",) + expert + ("tensor",), None),
        P(("dp",) + expert + ("tensor",), None),
        P(("dp",) + expert, None),
        P("dp", expert + ("tensor",)),
        P(None, expert + ("tensor",)),
    )
    out_specs = (
        P("dp", expert + ("tensor",)),
        P("dp", expert + ("tensor",)),
        P(("dp",) + expert + ("tensor",), None),
    )
    return jax.shard_map(shards, mesh=fine, in_specs=in_specs, out_specs=out_specs, check_vma=False)
```

```python
import functools

import jax
import jax.numpy as jnp
from jax import lax
from jax.experimental import pallas as pl
from jax.experimental.pallas import tpu as pltpu
from jax.sharding import Mesh, PartitionSpec as P

LANES = 128
SUBLANES = 8
PARTS = 3


def split3(value):
    high = value.astype(jnp.bfloat16)
    rest = value - high.astype(jnp.float32)
    middle = rest.astype(jnp.bfloat16)
    low = (rest - middle.astype(jnp.float32)).astype(jnp.bfloat16)
    return high, middle, low


def pack_kernel(cot_ref, probs_ref, out_ref):
    own_tokens, width = cot_ref.shape
    rest = own_tokens - SUBLANES
    piece = width // (PARTS + 1)
    out_ref[:, :width] = cot_ref[:SUBLANES, :]
    row = lax.broadcasted_iota(jnp.int32, (SUBLANES, own_tokens), 0)
    token = lax.broadcasted_iota(jnp.int32, (SUBLANES, own_tokens), 1)
    body = ((row < rest) & (token == SUBLANES + row)).astype(jnp.bfloat16)
    last = cot_ref[:, PARTS * piece :]
    for k in range(PARTS):
        source = SUBLANES + (row - rest) * PARTS + k
        tail = ((row >= rest) & (token == source)).astype(jnp.bfloat16)
        moved = jnp.dot(
            body, cot_ref[:, k * piece : (k + 1) * piece], preferred_element_type=jnp.float32
        ) + jnp.dot(tail, last, preferred_element_type=jnp.float32)
        start = width + k * piece
        out_ref[:, start : start + piece] = moved.astype(jnp.bfloat16)
    place = lax.axis_index("tensor") * own_tokens
    lane = lax.broadcasted_iota(jnp.int32, (own_tokens, LANES), 1)
    owner = lax.broadcasted_iota(jnp.int32, (own_tokens, LANES), 0)
    here = (lane == owner + place).astype(jnp.bfloat16)
    parts = [
        jnp.dot(part, here, preferred_element_type=jnp.float32) for part in split3(probs_ref[...])
    ]
    meta = jnp.concatenate(parts + [jnp.zeros((SUBLANES - 2 * PARTS, LANES), jnp.float32)], axis=0)
    out_ref[:, width + PARTS * piece :] = meta.astype(jnp.bfloat16)


def fill_kernel(own_tokens, experts, capacity, gathered_ref, ids_ref, out_ref):
    members = gathered_ref.shape[0]
    width = out_ref.shape[1]
    group = members * own_tokens
    rest = own_tokens - SUBLANES
    piece = width // (PARTS + 1)
    block = members * SUBLANES
    lane = lax.broadcasted_iota(jnp.int32, (group, LANES), 1)
    token = lax.broadcasted_iota(jnp.int32, (group, LANES), 0)
    moved = jnp.dot(
        ids_ref[...].astype(jnp.float32).astype(jnp.bfloat16),
        (lane == token).astype(jnp.bfloat16),
        preferred_element_type=jnp.float32,
    ).astype(jnp.int32)
    real = lax.broadcasted_iota(jnp.int32, (1, LANES), 1) < group
    spread = [jnp.where(real, moved[k : k + 1], -1) for k in range(2)]
    expert = lax.broadcasted_iota(jnp.int32, (experts, LANES), 0)
    named = [(spread[k] == expert).astype(jnp.float32) for k in range(2)]
    first = lax.broadcasted_iota(jnp.int32, (LANES, LANES), 0)
    second = lax.broadcasted_iota(jnp.int32, (LANES, LANES), 1)
    earlier = jnp.dot(
        (named[0] + named[1]).astype(jnp.bfloat16),
        (first < second).astype(jnp.bfloat16),
        preferred_element_type=jnp.float32,
    )
    meta = gathered_ref[:, :, width + PARTS * piece :].astype(jnp.float32)
    meta = jnp.sum(meta, axis=0)
    row = lax.broadcasted_iota(jnp.int32, (experts * capacity, LANES), 0)
    selector = jnp.zeros((experts * capacity, LANES), jnp.float32)
    weight = jnp.zeros((experts * capacity, LANES), jnp.float32)
    for k in range(2):
        count = earlier if k == 0 else earlier + named[0]
        slot = jnp.sum(count * named[k], axis=0, keepdims=True).astype(jnp.int32)
        key = jnp.where(spread[k] >= 0, spread[k] * capacity + slot, -1)
        prob = meta[k : k + 1] + meta[2 + k : 3 + k] + meta[4 + k : 5 + k]
        match = row == key
        selector = jnp.where(match, 1.0, selector)
        weight = jnp.where(match, prob, weight)
    scale = jnp.sum(weight, axis=1, keepdims=True)
    selector = selector.astype(jnp.bfloat16)

    region, within = second // block, second % SUBLANES
    base = ((second % block) // SUBLANES) * own_tokens
    head = jnp.where(region == 0, base + within, -1)
    body = jnp.where((region == 1) & (within < rest), base + SUBLANES + within, head)
    tail = base + SUBLANES + (within - rest) * PARTS + region - 1
    tail = jnp.where((region >= 1) & (within >= rest), tail, head)

    def picked(source):
        moved = jnp.dot(
            selector, (first == source).astype(jnp.bfloat16), preferred_element_type=jnp.float32
        )
        return moved.astype(jnp.bfloat16)

    picked_body, picked_tail = picked(body)[:, : 2 * block], picked(tail)

    def rows_at(start, step):
        rows = gathered_ref[:, :, start : start + step].astype(jnp.float32)
        return rows.reshape(block, step)

    step = 512
    for start in range(0, width, step):
        found = [rows_at(start, step)]
        if start < PARTS * piece:
            found.append(rows_at(width + start, step))
            chosen = picked_body
        else:
            for k in range(PARTS):
                found.append(rows_at(width + k * piece + start - PARTS * piece, step))
            chosen = picked_tail
        rows = jnp.dot(
            chosen,
            jnp.concatenate(found, axis=0).astype(jnp.bfloat16),
            preferred_element_type=jnp.float32,
        )
        out_ref[:, start : start + step] = (rows * scale).astype(jnp.bfloat16)


def parity_order(rows, capacity, from_natural):
    lanes = rows // 2
    axes = (0, 1) if from_natural else (1, 0)
    natural = lax.broadcasted_iota(jnp.int32, (rows, rows), axes[0])
    ordered = lax.broadcasted_iota(jnp.int32, (rows, rows), axes[1])
    here = lax.axis_index("par")
    parity = jnp.where(ordered < lanes, here, 1 - here)
    within = ordered % lanes
    source = (within // capacity) * (2 * capacity) + parity * capacity + within % capacity
    return (natural == source).astype(jnp.bfloat16)


def sort_kernel(capacity, hidden_ref, mine_ref, send_ref):
    rows = hidden_ref.shape[1]
    order = parity_order(rows, capacity, True)
    moved = jnp.dot(hidden_ref[...], order, preferred_element_type=jnp.float32)
    moved = moved.astype(jnp.bfloat16)
    mine_ref[...] = moved[:, : rows // 2]
    send_ref[...] = moved[:, rows // 2 :]


def product_kernel(
    capacity,
    rows_ref,
    weight_ref,
    weight_theirs_ref,
    hidden_ref,
    hidden_theirs_ref,
    mine_ref,
    theirs_ref,
    partial_ref,
    by_feature_ref,
    weight_buf,
    theirs_buf,
    turned,
    sems,
):
    replicas, cols, chunk = weight_theirs_ref.shape
    width = rows_ref.shape[1]
    cuts = (0, cols // 32 * 16, cols)
    weight_copies = [
        pltpu.make_async_copy(
            weight_ref.at[start:stop], weight_buf.at[start:stop], sems.at[0, index]
        )
        for index, (start, stop) in enumerate(zip(cuts[:-1], cuts[1:]))
    ]
    per = replicas // 4
    theirs_copies = [
        pltpu.make_async_copy(
            weight_theirs_ref.at[index * per : (index + 1) * per],
            theirs_buf.at[index * per : (index + 1) * per],
            sems.at[1, index],
        )
        for index in range(4)
    ]
    for copy in theirs_copies + weight_copies:
        copy.start()
    for index in range(replicas):
        rows = rows_ref[:, index * chunk : (index + 1) * chunk]
        by_feature_ref[index] = rows
        turned[index * chunk : (index + 1) * chunk, :] = rows.T
    theirs = jnp.zeros(theirs_ref.shape, jnp.float32)
    for index in range(4):
        theirs_copies[index].wait()
        for replica in range(index * per, (index + 1) * per):
            theirs += jnp.dot(
                theirs_buf[replica],
                turned[replica * chunk : (replica + 1) * chunk, :],
                preferred_element_type=jnp.float32,
            )
    mine = []
    for index, (start, stop) in enumerate(zip(cuts[:-1], cuts[1:])):
        weight_copies[index].wait()
        mine.append(
            jnp.dot(weight_buf[start:stop], turned[...], preferred_element_type=jnp.float32)
        )
    mine = jnp.concatenate(mine, axis=0)
    mine_ref[...] = mine.astype(jnp.bfloat16)
    theirs_ref[...] = theirs.astype(jnp.bfloat16)
    summed = jnp.sum(
        hidden_ref[...].astype(jnp.float32) * mine
        + hidden_theirs_ref[...].astype(jnp.float32) * theirs,
        axis=0,
        keepdims=True,
    )
    lanes = summed.shape[1]
    experts = partial_ref.shape[0]
    of_expert = lax.broadcasted_iota(jnp.int32, (experts, lanes), 1) // capacity
    expert = lax.broadcasted_iota(jnp.int32, (experts, lanes), 0)
    spread = jnp.where(of_expert == expert, summed, 0.0)
    at = lax.broadcasted_iota(jnp.int32, (lanes, LANES), 0) % capacity
    slot = lax.broadcasted_iota(jnp.int32, (lanes, LANES), 1)
    partial_ref[...] = jnp.dot(
        spread,
        (at == slot).astype(jnp.float32),
        precision=lax.Precision.HIGHEST,
        preferred_element_type=jnp.float32,
    )


def term_of(hidden_ref, rows_ref, half):
    replicas, depth, chunk = rows_ref.shape
    rows = rows_ref[...].reshape(replicas * depth, chunk)
    hidden = jnp.concatenate([hidden_ref[p, half] for p in range(replicas)], axis=1)
    return jnp.dot(hidden, rows, preferred_element_type=jnp.float32)


def send_kernel(hidden_ref, rows_ref, product_ref, out_ref):
    chunk = rows_ref.shape[2]
    out_ref[:, :chunk] = term_of(hidden_ref, rows_ref, 1).astype(jnp.bfloat16)
    out_ref[:, chunk:] = product_ref[...]


def keep_kernel(hidden_ref, rows_ref, out_ref):
    out_ref[...] = term_of(hidden_ref, rows_ref, 0)


def finish_kernel(capacity, term_ref, product_ref, swapped_ref, weight_ref, hidden_ref):
    chunk = term_ref.shape[1]
    term = term_ref[...] + swapped_ref[:, :chunk].astype(jnp.float32)
    weight_ref[...] = term.astype(jnp.bfloat16)
    order = parity_order(hidden_ref.shape[1], capacity, False)
    both = jnp.concatenate([product_ref[...], swapped_ref[:, chunk:]], axis=1)
    moved = jnp.dot(both, order, preferred_element_type=jnp.float32)
    hidden_ref[...] = moved.astype(jnp.bfloat16)


def assign_slots(flat_ids, experts):
    expert_range = jnp.arange(experts, dtype=jnp.int32)
    onehot = (flat_ids[:, None] == expert_range[None, :]).astype(jnp.int32)
    earlier = jnp.cumsum(onehot, axis=0) - onehot
    return jnp.sum(earlier * onehot, axis=1)


def windows(n_dp, n_y, n_q, n_par, n_tensor):
    groups = []
    for dp in range(n_dp):
        for par in range(n_par):
            for run in range(n_tensor):
                group = []
                for y in range(n_y):
                    for q in range(n_q):
                        wraps = dp % 2 == 1 and q < n_q // 2
                        at = (run + 1) % n_tensor if wraps else run
                        group.append((((dp * n_y + y) * n_q + q) * n_par + par) * n_tensor + at)
                groups.append(group)
    return groups


def shards(cotangent, probs, expert_ids, saved_hidden, down_weight):
    n_y, n_q, n_par = lax.axis_size("y"), lax.axis_size("zq"), lax.axis_size("par")
    members = lax.axis_size("tensor")
    n_expert = n_y * n_q * n_par
    experts = n_y * n_q
    own_tokens, model_width = cotangent.shape
    hidden_cols = saved_hidden.shape[1]
    capacity = saved_hidden.shape[0] // n_expert

    n_dp = lax.axis_size("dp")
    chunk = model_width // n_dp
    half = experts * capacity
    swap = [(0, 1), (1, 0)]
    small = pltpu.CompilerParams(vmem_limit_bytes=16 << 20)

    weight = down_weight.T
    weight_send = lax.dynamic_slice_in_dim(weight, lax.axis_index("dp") * chunk, chunk, axis=1)
    weight_swapped = lax.ppermute(weight_send, "par", swap)
    hidden_mine, hidden_send = pl.pallas_call(
        functools.partial(sort_kernel, capacity),
        out_shape=[jax.ShapeDtypeStruct((hidden_cols, half), jnp.bfloat16)] * 2,
        compiler_params=small,
    )(saved_hidden.T)
    hidden_theirs = lax.ppermute(hidden_send, "par", swap)
    packed_width = model_width + PARTS * model_width // (PARTS + 1) + LANES
    packed = pl.pallas_call(
        pack_kernel,
        out_shape=jax.ShapeDtypeStruct((SUBLANES, packed_width), jnp.bfloat16),
        compiler_params=small,
    )(cotangent, probs.T)
    packed, weight_swapped = lax.optimization_barrier((packed, weight_swapped))
    weight_theirs = lax.all_gather(weight_swapped, "dp", axis=0)
    hidden_all = lax.all_gather(jnp.stack([hidden_mine, hidden_theirs]), "dp", axis=0)

    gathered = lax.all_gather(packed, "tensor", axis=0)
    buffer = pl.pallas_call(
        functools.partial(fill_kernel, own_tokens, experts, capacity),
        out_shape=jax.ShapeDtypeStruct((half, model_width), jnp.bfloat16),
        compiler_params=pltpu.CompilerParams(vmem_limit_bytes=24 << 20),
    )(gathered, expert_ids.T)
    buffer, weight_theirs = lax.optimization_barrier((buffer, weight_theirs))
    buffer = buffer.reshape(experts, capacity, model_width)
    groups = windows(n_dp, n_y, n_q, n_par, members)
    every = ("dp", "y", "zq", "par", "tensor")
    rows = lax.all_to_all(
        buffer, every, split_axis=0, concat_axis=0, axis_index_groups=groups, tiled=True
    ).reshape(half, model_width)

    flat_ids = expert_ids.reshape(-1)
    keys = flat_ids * capacity + assign_slots(flat_ids, experts)
    start_row = lax.axis_index("tensor") * (own_tokens * 2)
    own_keys = lax.dynamic_slice_in_dim(keys, start_row, own_tokens * 2)
    rows, own_keys = lax.optimization_barrier((rows, own_keys))

    vmem = pl.BlockSpec(memory_space=pltpu.VMEM)
    hbm = pl.BlockSpec(memory_space=pltpu.HBM)
    product, product_theirs, partial_value, by_feature = pl.pallas_call(
        functools.partial(product_kernel, capacity),
        in_specs=[vmem, hbm, hbm, vmem, vmem],
        out_specs=[vmem] * 4,
        out_shape=[
            jax.ShapeDtypeStruct((hidden_cols, half), jnp.bfloat16),
            jax.ShapeDtypeStruct((hidden_cols, half), jnp.bfloat16),
            jax.ShapeDtypeStruct((experts, LANES), jnp.float32),
            jax.ShapeDtypeStruct((n_dp, half, chunk), jnp.bfloat16),
        ],
        scratch_shapes=[
            pltpu.VMEM((hidden_cols, model_width), jnp.bfloat16),
            pltpu.VMEM((n_dp, hidden_cols, chunk), jnp.bfloat16),
            pltpu.VMEM((model_width, half), jnp.bfloat16),
            pltpu.SemaphoreType.DMA((2, 4)),
        ],
        compiler_params=pltpu.CompilerParams(vmem_limit_bytes=50 << 20),
    )(rows, weight, weight_theirs, hidden_mine, hidden_theirs)

    replica_rows = lax.all_to_all(by_feature, "dp", split_axis=0, concat_axis=0, tiled=True)
    partial_value = lax.psum(partial_value, "tensor")
    partial_value, replica_rows = lax.optimization_barrier((partial_value, replica_rows))
    term_cost = pl.CostEstimate(
        flops=2 * n_dp * half * hidden_cols * chunk,
        bytes_accessed=2 * n_dp * half * (hidden_cols + chunk) + 4 * hidden_cols * chunk,
        transcendentals=0,
    )
    medium = pltpu.CompilerParams(vmem_limit_bytes=50 << 20)
    sent = pl.pallas_call(
        send_kernel,
        out_shape=jax.ShapeDtypeStruct((hidden_cols, chunk + half), jnp.bfloat16),
        cost_estimate=term_cost,
        compiler_params=medium,
    )(hidden_all, replica_rows, product_theirs)
    swapped = lax.ppermute(sent, "par", swap)
    term = pl.pallas_call(
        keep_kernel,
        out_shape=jax.ShapeDtypeStruct((hidden_cols, chunk), jnp.float32),
        cost_estimate=term_cost,
        compiler_params=medium,
    )(hidden_all, replica_rows)
    weight_grad, hidden_grad = pl.pallas_call(
        functools.partial(finish_kernel, capacity),
        out_shape=[
            jax.ShapeDtypeStruct((hidden_cols, chunk), jnp.bfloat16),
            jax.ShapeDtypeStruct((hidden_cols, 2 * half), jnp.bfloat16),
        ],
        compiler_params=medium,
    )(term, product, swapped)
    weight_grad, hidden_grad = weight_grad.T, hidden_grad.T
    lookup = lax.all_to_all(
        partial_value, every, split_axis=0, concat_axis=0, axis_index_groups=groups, tiled=True
    )

    expert = lax.broadcasted_iota(jnp.int32, (1, experts, LANES), 1)
    slot = lax.broadcasted_iota(jnp.int32, (1, experts, LANES), 2)
    chosen = (own_keys[:, None, None] == expert * capacity + slot) & (slot < capacity)
    values = jnp.sum(jnp.where(chosen, lookup[None], 0.0), axis=(1, 2)).reshape(own_tokens, 2)
    prob_grad = values / probs
    return (hidden_grad, weight_grad, prob_grad)


def solution(mesh):
    n_dp, n_expert, n_tensor = mesh.devices.shape
    fine = Mesh(
        mesh.devices.reshape(n_dp, 4, n_expert // 8, 2, n_tensor), ("dp", "y", "zq", "par", "tensor")
    )
    expert = ("y", "zq", "par")
    in_specs = (
        P(("dp",) + expert + ("tensor",), None),
        P(("dp",) + expert + ("tensor",), None),
        P(("dp",) + expert, None),
        P("dp", expert + ("tensor",)),
        P(None, expert + ("tensor",)),
    )
    out_specs = (
        P("dp", expert + ("tensor",)),
        P("dp", expert + ("tensor",)),
        P(("dp",) + expert + ("tensor",), None),
    )
    return jax.shard_map(shards, mesh=fine, in_specs=in_specs, out_specs=out_specs, check_vma=False)
```

```python
import functools

import jax
import jax.numpy as jnp
from jax import lax
from jax.experimental import pallas as pl
from jax.experimental.pallas import tpu as pltpu
from jax.sharding import Mesh, PartitionSpec as P

LANES = 128
SUBLANES = 8
PARTS = 3


def split3(value):
    high = value.astype(jnp.bfloat16)
    rest = value - high.astype(jnp.float32)
    middle = rest.astype(jnp.bfloat16)
    low = (rest - middle.astype(jnp.float32)).astype(jnp.bfloat16)
    return high, middle, low


def pack_kernel(cot_ref, probs_ref, out_ref):
    own_tokens, width = cot_ref.shape
    rest = own_tokens - SUBLANES
    piece = width // (PARTS + 1)
    out_ref[:, :width] = cot_ref[:SUBLANES, :]
    row = lax.broadcasted_iota(jnp.int32, (SUBLANES, own_tokens), 0)
    token = lax.broadcasted_iota(jnp.int32, (SUBLANES, own_tokens), 1)
    body = ((row < rest) & (token == SUBLANES + row)).astype(jnp.bfloat16)
    last = cot_ref[:, PARTS * piece :]
    for k in range(PARTS):
        source = SUBLANES + (row - rest) * PARTS + k
        tail = ((row >= rest) & (token == source)).astype(jnp.bfloat16)
        moved = jnp.dot(
            body, cot_ref[:, k * piece : (k + 1) * piece], preferred_element_type=jnp.float32
        ) + jnp.dot(tail, last, preferred_element_type=jnp.float32)
        start = width + k * piece
        out_ref[:, start : start + piece] = moved.astype(jnp.bfloat16)
    place = lax.axis_index("tensor") * own_tokens
    lane = lax.broadcasted_iota(jnp.int32, (own_tokens, LANES), 1)
    owner = lax.broadcasted_iota(jnp.int32, (own_tokens, LANES), 0)
    here = (lane == owner + place).astype(jnp.bfloat16)
    parts = [
        jnp.dot(part, here, preferred_element_type=jnp.float32) for part in split3(probs_ref[...])
    ]
    meta = jnp.concatenate(parts + [jnp.zeros((SUBLANES - 2 * PARTS, LANES), jnp.float32)], axis=0)
    out_ref[:, width + PARTS * piece :] = meta.astype(jnp.bfloat16)


def fill_kernel(own_tokens, experts, capacity, gathered_ref, ids_ref, out_ref):
    members = gathered_ref.shape[0]
    width = out_ref.shape[1]
    group = members * own_tokens
    rest = own_tokens - SUBLANES
    piece = width // (PARTS + 1)
    block = members * SUBLANES
    lane = lax.broadcasted_iota(jnp.int32, (group, LANES), 1)
    token = lax.broadcasted_iota(jnp.int32, (group, LANES), 0)
    moved = jnp.dot(
        ids_ref[...].astype(jnp.float32).astype(jnp.bfloat16),
        (lane == token).astype(jnp.bfloat16),
        preferred_element_type=jnp.float32,
    ).astype(jnp.int32)
    real = lax.broadcasted_iota(jnp.int32, (1, LANES), 1) < group
    spread = [jnp.where(real, moved[k : k + 1], -1) for k in range(2)]
    expert = lax.broadcasted_iota(jnp.int32, (experts, LANES), 0)
    named = [(spread[k] == expert).astype(jnp.float32) for k in range(2)]
    first = lax.broadcasted_iota(jnp.int32, (LANES, LANES), 0)
    second = lax.broadcasted_iota(jnp.int32, (LANES, LANES), 1)
    earlier = jnp.dot(
        (named[0] + named[1]).astype(jnp.bfloat16),
        (first < second).astype(jnp.bfloat16),
        preferred_element_type=jnp.float32,
    )
    meta = gathered_ref[:, :, width + PARTS * piece :].astype(jnp.float32)
    meta = jnp.sum(meta, axis=0)
    row = lax.broadcasted_iota(jnp.int32, (experts * capacity, LANES), 0)
    selector = jnp.zeros((experts * capacity, LANES), jnp.float32)
    weight = jnp.zeros((experts * capacity, LANES), jnp.float32)
    for k in range(2):
        count = earlier if k == 0 else earlier + named[0]
        slot = jnp.sum(count * named[k], axis=0, keepdims=True).astype(jnp.int32)
        key = jnp.where(spread[k] >= 0, spread[k] * capacity + slot, -1)
        prob = meta[k : k + 1] + meta[2 + k : 3 + k] + meta[4 + k : 5 + k]
        match = row == key
        selector = jnp.where(match, 1.0, selector)
        weight = jnp.where(match, prob, weight)
    scale = jnp.sum(weight, axis=1, keepdims=True)
    selector = selector.astype(jnp.bfloat16)

    region, within = second // block, second % SUBLANES
    base = ((second % block) // SUBLANES) * own_tokens
    head = jnp.where(region == 0, base + within, -1)
    body = jnp.where((region == 1) & (within < rest), base + SUBLANES + within, head)
    tail = base + SUBLANES + (within - rest) * PARTS + region - 1
    tail = jnp.where((region >= 1) & (within >= rest), tail, head)

    def picked(source):
        moved = jnp.dot(
            selector, (first == source).astype(jnp.bfloat16), preferred_element_type=jnp.float32
        )
        return moved.astype(jnp.bfloat16)

    picked_body, picked_tail = picked(body)[:, : 2 * block], picked(tail)

    def rows_at(start, step):
        rows = gathered_ref[:, :, start : start + step].astype(jnp.float32)
        return rows.reshape(block, step)

    step = 512
    for start in range(0, width, step):
        found = [rows_at(start, step)]
        if start < PARTS * piece:
            found.append(rows_at(width + start, step))
            chosen = picked_body
        else:
            for k in range(PARTS):
                found.append(rows_at(width + k * piece + start - PARTS * piece, step))
            chosen = picked_tail
        rows = jnp.dot(
            chosen,
            jnp.concatenate(found, axis=0).astype(jnp.bfloat16),
            preferred_element_type=jnp.float32,
        )
        out_ref[:, start : start + step] = (rows * scale).astype(jnp.bfloat16)


def parity_order(rows, capacity, from_natural):
    lanes = rows // 2
    axes = (0, 1) if from_natural else (1, 0)
    natural = lax.broadcasted_iota(jnp.int32, (rows, rows), axes[0])
    ordered = lax.broadcasted_iota(jnp.int32, (rows, rows), axes[1])
    here = lax.axis_index("par")
    parity = jnp.where(ordered < lanes, here, 1 - here)
    within = ordered % lanes
    source = (within // capacity) * (2 * capacity) + parity * capacity + within % capacity
    return (natural == source).astype(jnp.bfloat16)


def prepare_kernel(capacity, weight_ref, hidden_ref, send_ref, mine_ref, sem):
    rows = hidden_ref.shape[1]
    chunk = send_ref.shape[1] - rows // 2
    start = pl.multiple_of(lax.axis_index("dp") * chunk, chunk)
    copy = pltpu.make_async_copy(
        weight_ref.at[:, pl.ds(start, chunk)], send_ref.at[:, :chunk], sem
    )
    copy.start()
    order = parity_order(rows, capacity, True)
    moved = jnp.dot(hidden_ref[...], order, preferred_element_type=jnp.float32)
    moved = moved.astype(jnp.bfloat16)
    mine_ref[...] = moved[:, : rows // 2]
    send_ref[:, chunk:] = moved[:, rows // 2 :]
    copy.wait()


def product_kernel(
    capacity,
    rows_ref,
    weight_ref,
    weight_theirs_ref,
    hidden_ref,
    hidden_theirs_ref,
    mine_ref,
    theirs_ref,
    partial_ref,
    by_feature_ref,
    weight_buf,
    theirs_buf,
    turned,
    sems,
):
    replicas, cols, chunk = theirs_buf.shape
    cuts = (0, cols // 32 * 16, cols)
    weight_copies = [
        pltpu.make_async_copy(
            weight_ref.at[start:stop], weight_buf.at[start:stop], sems.at[0, index]
        )
        for index, (start, stop) in enumerate(zip(cuts[:-1], cuts[1:]))
    ]
    per = replicas // 4
    theirs_copies = [
        pltpu.make_async_copy(
            weight_theirs_ref.at[index * per : (index + 1) * per, :, :chunk],
            theirs_buf.at[index * per : (index + 1) * per],
            sems.at[1, index],
        )
        for index in range(4)
    ]
    for copy in theirs_copies + weight_copies:
        copy.start()
    for index in range(replicas):
        rows = rows_ref[:, index * chunk : (index + 1) * chunk]
        by_feature_ref[index] = rows
        turned[index * chunk : (index + 1) * chunk, :] = rows.T
    theirs = jnp.zeros(theirs_ref.shape, jnp.float32)
    for index in range(4):
        theirs_copies[index].wait()
        for replica in range(index * per, (index + 1) * per):
            theirs += jnp.dot(
                theirs_buf[replica],
                turned[replica * chunk : (replica + 1) * chunk, :],
                preferred_element_type=jnp.float32,
            )
    mine = []
    for index, (start, stop) in enumerate(zip(cuts[:-1], cuts[1:])):
        weight_copies[index].wait()
        mine.append(
            jnp.dot(weight_buf[start:stop], turned[...], preferred_element_type=jnp.float32)
        )
    mine = jnp.concatenate(mine, axis=0)
    mine_ref[...] = mine.astype(jnp.bfloat16)
    theirs_ref[...] = theirs.astype(jnp.bfloat16)
    summed = jnp.sum(
        hidden_ref[...].astype(jnp.float32) * mine
        + hidden_theirs_ref[...].astype(jnp.float32) * theirs,
        axis=0,
        keepdims=True,
    )
    lanes = summed.shape[1]
    experts = partial_ref.shape[0]
    of_expert = lax.broadcasted_iota(jnp.int32, (experts, lanes), 1) // capacity
    expert = lax.broadcasted_iota(jnp.int32, (experts, lanes), 0)
    spread = jnp.where(of_expert == expert, summed, 0.0)
    at = lax.broadcasted_iota(jnp.int32, (lanes, LANES), 0) % capacity
    slot = lax.broadcasted_iota(jnp.int32, (lanes, LANES), 1)
    partial_ref[...] = jnp.dot(
        spread,
        (at == slot).astype(jnp.float32),
        precision=lax.Precision.HIGHEST,
        preferred_element_type=jnp.float32,
    )


def term_of(hidden_ref, rows_ref, half):
    replicas, depth, chunk = rows_ref.shape
    rows = rows_ref[...].reshape(replicas * depth, chunk)
    lanes = slice(half * depth, (half + 1) * depth)
    hidden = jnp.concatenate([hidden_ref[p, :, lanes] for p in range(replicas)], axis=1)
    return jnp.dot(hidden, rows, preferred_element_type=jnp.float32)


def send_kernel(hidden_ref, rows_ref, product_ref, out_ref):
    chunk = rows_ref.shape[2]
    out_ref[:, :chunk] = term_of(hidden_ref, rows_ref, 0).astype(jnp.bfloat16)
    out_ref[:, chunk:] = product_ref[...]


def keep_kernel(hidden_ref, rows_ref, out_ref):
    out_ref[...] = term_of(hidden_ref, rows_ref, 1)


def finish_kernel(capacity, term_ref, product_ref, swapped_ref, weight_ref, hidden_ref):
    chunk = term_ref.shape[1]
    term = term_ref[...] + swapped_ref[:, :chunk].astype(jnp.float32)
    weight_ref[...] = term.astype(jnp.bfloat16)
    order = parity_order(hidden_ref.shape[1], capacity, False)
    both = jnp.concatenate([product_ref[...], swapped_ref[:, chunk:]], axis=1)
    moved = jnp.dot(both, order, preferred_element_type=jnp.float32)
    hidden_ref[...] = moved.astype(jnp.bfloat16)


def assign_slots(flat_ids, experts):
    expert_range = jnp.arange(experts, dtype=jnp.int32)
    onehot = (flat_ids[:, None] == expert_range[None, :]).astype(jnp.int32)
    earlier = jnp.cumsum(onehot, axis=0) - onehot
    return jnp.sum(earlier * onehot, axis=1)


def windows(n_dp, n_y, n_q, n_par, n_tensor):
    groups = []
    for dp in range(n_dp):
        for par in range(n_par):
            for run in range(n_tensor):
                group = []
                for y in range(n_y):
                    for q in range(n_q):
                        wraps = dp % 2 == 1 and q < n_q // 2
                        at = (run + 1) % n_tensor if wraps else run
                        group.append((((dp * n_y + y) * n_q + q) * n_par + par) * n_tensor + at)
                groups.append(group)
    return groups


def shards(cotangent, probs, expert_ids, saved_hidden, down_weight):
    n_y, n_q, n_par = lax.axis_size("y"), lax.axis_size("zq"), lax.axis_size("par")
    members = lax.axis_size("tensor")
    n_expert = n_y * n_q * n_par
    experts = n_y * n_q
    own_tokens, model_width = cotangent.shape
    hidden_cols = saved_hidden.shape[1]
    capacity = saved_hidden.shape[0] // n_expert

    n_dp = lax.axis_size("dp")
    chunk = model_width // n_dp
    half = experts * capacity
    swap = [(0, 1), (1, 0)]
    large = pltpu.CompilerParams(vmem_limit_bytes=50 << 20)
    small = pltpu.CompilerParams(vmem_limit_bytes=16 << 20)

    weight = down_weight.T
    vmem = pl.BlockSpec(memory_space=pltpu.VMEM)
    hbm = pl.BlockSpec(memory_space=pltpu.HBM)
    sent, hidden_mine = pl.pallas_call(
        functools.partial(prepare_kernel, capacity),
        in_specs=[hbm, vmem],
        out_specs=[vmem, vmem],
        out_shape=[
            jax.ShapeDtypeStruct((hidden_cols, chunk + half), jnp.bfloat16),
            jax.ShapeDtypeStruct((hidden_cols, half), jnp.bfloat16),
        ],
        scratch_shapes=[pltpu.SemaphoreType.DMA],
        compiler_params=large,
    )(weight, saved_hidden.T)
    swapped = lax.ppermute(sent, "par", swap)
    packed_width = model_width + PARTS * model_width // (PARTS + 1) + LANES
    packed = pl.pallas_call(
        pack_kernel,
        out_shape=jax.ShapeDtypeStruct((SUBLANES, packed_width), jnp.bfloat16),
        compiler_params=small,
    )(cotangent, probs.T)
    flat_ids = expert_ids.reshape(-1)
    keys = flat_ids * capacity + assign_slots(flat_ids, experts)
    start_row = lax.axis_index("tensor") * (own_tokens * 2)
    own_keys = lax.dynamic_slice_in_dim(keys, start_row, own_tokens * 2)
    packed, swapped, own_keys = lax.optimization_barrier((packed, swapped, own_keys))
    prefetched = lax.all_gather(jnp.concatenate([swapped, hidden_mine], axis=1), "dp", axis=0)

    gathered = lax.all_gather(packed, "tensor", axis=0)
    buffer = pl.pallas_call(
        functools.partial(fill_kernel, own_tokens, experts, capacity),
        out_shape=jax.ShapeDtypeStruct((half, model_width), jnp.bfloat16),
        compiler_params=pltpu.CompilerParams(vmem_limit_bytes=24 << 20),
    )(gathered, expert_ids.T)
    buffer = buffer.reshape(experts, capacity, model_width)
    groups = windows(n_dp, n_y, n_q, n_par, members)
    every = ("dp", "y", "zq", "par", "tensor")
    rows = lax.all_to_all(
        buffer, every, split_axis=0, concat_axis=0, axis_index_groups=groups, tiled=True
    ).reshape(half, model_width)

    product, product_theirs, partial_value, by_feature = pl.pallas_call(
        functools.partial(product_kernel, capacity),
        grid=(1,),
        in_specs=[
            vmem,
            hbm,
            hbm,
            vmem,
            pl.BlockSpec((hidden_cols, half), lambda i: (0, chunk // half)),
        ],
        out_specs=[vmem] * 4,
        out_shape=[
            jax.ShapeDtypeStruct((hidden_cols, half), jnp.bfloat16),
            jax.ShapeDtypeStruct((hidden_cols, half), jnp.bfloat16),
            jax.ShapeDtypeStruct((experts, LANES), jnp.float32),
            jax.ShapeDtypeStruct((n_dp, half, chunk), jnp.bfloat16),
        ],
        scratch_shapes=[
            pltpu.VMEM((hidden_cols, model_width), jnp.bfloat16),
            pltpu.VMEM((n_dp, hidden_cols, chunk), jnp.bfloat16),
            pltpu.VMEM((model_width, half), jnp.bfloat16),
            pltpu.SemaphoreType.DMA((2, 4)),
        ],
        compiler_params=pltpu.CompilerParams(vmem_limit_bytes=50 << 20),
    )(rows, weight, prefetched, hidden_mine, swapped)

    replica_rows = lax.all_to_all(by_feature, "dp", split_axis=0, concat_axis=0, tiled=True)
    partial_value = lax.psum(partial_value, "tensor")
    partial_value, replica_rows = lax.optimization_barrier((partial_value, replica_rows))
    term_cost = pl.CostEstimate(
        flops=2 * n_dp * half * hidden_cols * chunk,
        bytes_accessed=2 * n_dp * half * (hidden_cols + chunk) + 4 * hidden_cols * chunk,
        transcendentals=0,
    )
    medium = pltpu.CompilerParams(vmem_limit_bytes=50 << 20)
    saved = pl.BlockSpec((n_dp, hidden_cols, 2 * half), lambda i: (0, 0, chunk // (2 * half)))
    sent = pl.pallas_call(
        send_kernel,
        grid=(1,),
        in_specs=[saved, vmem, vmem],
        out_shape=jax.ShapeDtypeStruct((hidden_cols, chunk + half), jnp.bfloat16),
        cost_estimate=term_cost,
        compiler_params=medium,
    )(prefetched, replica_rows, product_theirs)
    swapped = lax.ppermute(sent, "par", swap)
    term = pl.pallas_call(
        keep_kernel,
        grid=(1,),
        in_specs=[saved, vmem],
        out_shape=jax.ShapeDtypeStruct((hidden_cols, chunk), jnp.float32),
        cost_estimate=term_cost,
        compiler_params=medium,
    )(prefetched, replica_rows)
    weight_grad, hidden_grad = pl.pallas_call(
        functools.partial(finish_kernel, capacity),
        out_shape=[
            jax.ShapeDtypeStruct((hidden_cols, chunk), jnp.bfloat16),
            jax.ShapeDtypeStruct((hidden_cols, 2 * half), jnp.bfloat16),
        ],
        compiler_params=medium,
    )(term, product, swapped)
    weight_grad, hidden_grad = weight_grad.T, hidden_grad.T
    lookup = lax.all_to_all(
        partial_value, every, split_axis=0, concat_axis=0, axis_index_groups=groups, tiled=True
    )

    expert = lax.broadcasted_iota(jnp.int32, (1, experts, LANES), 1)
    slot = lax.broadcasted_iota(jnp.int32, (1, experts, LANES), 2)
    chosen = (own_keys[:, None, None] == expert * capacity + slot) & (slot < capacity)
    values = jnp.sum(jnp.where(chosen, lookup[None], 0.0), axis=(1, 2)).reshape(own_tokens, 2)
    prob_grad = values / probs
    return (hidden_grad, weight_grad, prob_grad)


def solution(mesh):
    n_dp, n_expert, n_tensor = mesh.devices.shape
    fine = Mesh(
        mesh.devices.reshape(n_dp, 4, n_expert // 8, 2, n_tensor), ("dp", "y", "zq", "par", "tensor")
    )
    expert = ("y", "zq", "par")
    in_specs = (
        P(("dp",) + expert + ("tensor",), None),
        P(("dp",) + expert + ("tensor",), None),
        P(("dp",) + expert, None),
        P("dp", expert + ("tensor",)),
        P(None, expert + ("tensor",)),
    )
    out_specs = (
        P("dp", expert + ("tensor",)),
        P("dp", expert + ("tensor",)),
        P(("dp",) + expert + ("tensor",), None),
    )
    return jax.shard_map(shards, mesh=fine, in_specs=in_specs, out_specs=out_specs, check_vma=False)
```

```python
import functools

import jax
import jax.numpy as jnp
from jax import lax
from jax.experimental import pallas as pl
from jax.experimental.pallas import tpu as pltpu
from jax.sharding import Mesh, PartitionSpec as P

LANES = 128
SUBLANES = 8
PARTS = 3


def split3(value):
    high = value.astype(jnp.bfloat16)
    rest = value - high.astype(jnp.float32)
    middle = rest.astype(jnp.bfloat16)
    low = (rest - middle.astype(jnp.float32)).astype(jnp.bfloat16)
    return high, middle, low


def pack_kernel(cot_ref, probs_ref, out_ref):
    own_tokens, width = cot_ref.shape
    rest = own_tokens - SUBLANES
    piece = width // (PARTS + 1)
    out_ref[:, :width] = cot_ref[:SUBLANES, :]
    row = lax.broadcasted_iota(jnp.int32, (SUBLANES, own_tokens), 0)
    token = lax.broadcasted_iota(jnp.int32, (SUBLANES, own_tokens), 1)
    body = ((row < rest) & (token == SUBLANES + row)).astype(jnp.bfloat16)
    last = cot_ref[:, PARTS * piece :]
    for k in range(PARTS):
        source = SUBLANES + (row - rest) * PARTS + k
        tail = ((row >= rest) & (token == source)).astype(jnp.bfloat16)
        moved = jnp.dot(
            body, cot_ref[:, k * piece : (k + 1) * piece], preferred_element_type=jnp.float32
        ) + jnp.dot(tail, last, preferred_element_type=jnp.float32)
        start = width + k * piece
        out_ref[:, start : start + piece] = moved.astype(jnp.bfloat16)
    place = lax.axis_index("tensor") * own_tokens
    lane = lax.broadcasted_iota(jnp.int32, (own_tokens, LANES), 1)
    owner = lax.broadcasted_iota(jnp.int32, (own_tokens, LANES), 0)
    here = (lane == owner + place).astype(jnp.bfloat16)
    parts = [
        jnp.dot(part, here, preferred_element_type=jnp.float32) for part in split3(probs_ref[...])
    ]
    meta = jnp.concatenate(parts + [jnp.zeros((SUBLANES - 2 * PARTS, LANES), jnp.float32)], axis=0)
    out_ref[:, width + PARTS * piece :] = meta.astype(jnp.bfloat16)


def fill_kernel(own_tokens, experts, capacity, gathered_ref, ids_ref, out_ref):
    members = gathered_ref.shape[0]
    width = out_ref.shape[1]
    group = members * own_tokens
    rest = own_tokens - SUBLANES
    piece = width // (PARTS + 1)
    block = members * SUBLANES
    lane = lax.broadcasted_iota(jnp.int32, (group, LANES), 1)
    token = lax.broadcasted_iota(jnp.int32, (group, LANES), 0)
    moved = jnp.dot(
        ids_ref[...].astype(jnp.float32).astype(jnp.bfloat16),
        (lane == token).astype(jnp.bfloat16),
        preferred_element_type=jnp.float32,
    ).astype(jnp.int32)
    real = lax.broadcasted_iota(jnp.int32, (1, LANES), 1) < group
    spread = [jnp.where(real, moved[k : k + 1], -1) for k in range(2)]
    expert = lax.broadcasted_iota(jnp.int32, (experts, LANES), 0)
    named = [(spread[k] == expert).astype(jnp.float32) for k in range(2)]
    first = lax.broadcasted_iota(jnp.int32, (LANES, LANES), 0)
    second = lax.broadcasted_iota(jnp.int32, (LANES, LANES), 1)
    earlier = jnp.dot(
        (named[0] + named[1]).astype(jnp.bfloat16),
        (first < second).astype(jnp.bfloat16),
        preferred_element_type=jnp.float32,
    )
    meta = gathered_ref[:, :, width + PARTS * piece :].astype(jnp.float32)
    meta = jnp.sum(meta, axis=0)
    row = lax.broadcasted_iota(jnp.int32, (experts * capacity, LANES), 0)
    selector = jnp.zeros((experts * capacity, LANES), jnp.float32)
    weight = jnp.zeros((experts * capacity, LANES), jnp.float32)
    for k in range(2):
        count = earlier if k == 0 else earlier + named[0]
        slot = jnp.sum(count * named[k], axis=0, keepdims=True).astype(jnp.int32)
        key = jnp.where(spread[k] >= 0, spread[k] * capacity + slot, -1)
        prob = meta[k : k + 1] + meta[2 + k : 3 + k] + meta[4 + k : 5 + k]
        match = row == key
        selector = jnp.where(match, 1.0, selector)
        weight = jnp.where(match, prob, weight)
    scale = jnp.sum(weight, axis=1, keepdims=True)
    selector = selector.astype(jnp.bfloat16)

    region, within = second // block, second % SUBLANES
    base = ((second % block) // SUBLANES) * own_tokens
    head = jnp.where(region == 0, base + within, -1)
    body = jnp.where((region == 1) & (within < rest), base + SUBLANES + within, head)
    tail = base + SUBLANES + (within - rest) * PARTS + region - 1
    tail = jnp.where((region >= 1) & (within >= rest), tail, head)

    def picked(source):
        moved = jnp.dot(
            selector, (first == source).astype(jnp.bfloat16), preferred_element_type=jnp.float32
        )
        return moved.astype(jnp.bfloat16)

    picked_body, picked_tail = picked(body)[:, : 2 * block], picked(tail)

    def rows_at(start, step):
        rows = gathered_ref[:, :, start : start + step].astype(jnp.float32)
        return rows.reshape(block, step)

    step = 512
    for start in range(0, width, step):
        found = [rows_at(start, step)]
        if start < PARTS * piece:
            found.append(rows_at(width + start, step))
            chosen = picked_body
        else:
            for k in range(PARTS):
                found.append(rows_at(width + k * piece + start - PARTS * piece, step))
            chosen = picked_tail
        rows = jnp.dot(
            chosen,
            jnp.concatenate(found, axis=0).astype(jnp.bfloat16),
            preferred_element_type=jnp.float32,
        )
        out_ref[:, start : start + step] = (rows * scale).astype(jnp.bfloat16)


def parity_order(rows, capacity, from_natural):
    lanes = rows // 2
    axes = (0, 1) if from_natural else (1, 0)
    natural = lax.broadcasted_iota(jnp.int32, (rows, rows), axes[0])
    ordered = lax.broadcasted_iota(jnp.int32, (rows, rows), axes[1])
    here = lax.axis_index("par")
    parity = jnp.where(ordered < lanes, here, 1 - here)
    within = ordered % lanes
    source = (within // capacity) * (2 * capacity) + parity * capacity + within % capacity
    return (natural == source).astype(jnp.bfloat16)


def prepare_kernel(capacity, weight_ref, hidden_ref, send_ref, mine_ref, sem):
    rows = hidden_ref.shape[1]
    chunk = send_ref.shape[1] - rows // 2
    start = pl.multiple_of(lax.axis_index("dp") * chunk, chunk)
    copy = pltpu.make_async_copy(
        weight_ref.at[:, pl.ds(start, chunk)], send_ref.at[:, :chunk], sem
    )
    copy.start()
    order = parity_order(rows, capacity, True)
    moved = jnp.dot(hidden_ref[...], order, preferred_element_type=jnp.float32)
    moved = moved.astype(jnp.bfloat16)
    mine_ref[...] = moved[:, : rows // 2]
    send_ref[:, chunk:] = moved[:, rows // 2 :]
    copy.wait()


def product_kernel(
    capacity,
    rows_ref,
    weight_ref,
    weight_theirs_ref,
    hidden_ref,
    hidden_theirs_ref,
    mine_ref,
    theirs_ref,
    partial_ref,
    by_feature_ref,
    weight_buf,
    theirs_buf,
    turned,
    sems,
):
    replicas, cols, chunk = theirs_buf.shape
    cuts = (0, cols // 32 * 16, cols)
    weight_copies = [
        pltpu.make_async_copy(
            weight_ref.at[start:stop], weight_buf.at[start:stop], sems.at[0, index]
        )
        for index, (start, stop) in enumerate(zip(cuts[:-1], cuts[1:]))
    ]
    per = replicas // 4
    theirs_copies = [
        pltpu.make_async_copy(
            weight_theirs_ref.at[index * per : (index + 1) * per, :, :chunk],
            theirs_buf.at[index * per : (index + 1) * per],
            sems.at[1, index],
        )
        for index in range(4)
    ]
    for copy in theirs_copies + weight_copies:
        copy.start()
    for index in range(replicas):
        rows = rows_ref[:, index * chunk : (index + 1) * chunk]
        by_feature_ref[index] = rows
        turned[index * chunk : (index + 1) * chunk, :] = rows.T
    theirs = jnp.zeros(theirs_ref.shape, jnp.float32)
    for index in range(4):
        theirs_copies[index].wait()
        for replica in range(index * per, (index + 1) * per):
            theirs += jnp.dot(
                theirs_buf[replica],
                turned[replica * chunk : (replica + 1) * chunk, :],
                preferred_element_type=jnp.float32,
            )
    mine = []
    for index, (start, stop) in enumerate(zip(cuts[:-1], cuts[1:])):
        weight_copies[index].wait()
        mine.append(
            jnp.dot(weight_buf[start:stop], turned[...], preferred_element_type=jnp.float32)
        )
    mine = jnp.concatenate(mine, axis=0)
    mine_ref[...] = mine.astype(jnp.bfloat16)
    theirs_ref[...] = theirs.astype(jnp.bfloat16)
    summed = jnp.sum(
        hidden_ref[...].astype(jnp.float32) * mine
        + hidden_theirs_ref[...].astype(jnp.float32) * theirs,
        axis=0,
        keepdims=True,
    )
    lanes = summed.shape[1]
    experts = partial_ref.shape[0]
    of_expert = lax.broadcasted_iota(jnp.int32, (experts, lanes), 1) // capacity
    expert = lax.broadcasted_iota(jnp.int32, (experts, lanes), 0)
    spread = jnp.where(of_expert == expert, summed, 0.0)
    at = lax.broadcasted_iota(jnp.int32, (lanes, LANES), 0) % capacity
    slot = lax.broadcasted_iota(jnp.int32, (lanes, LANES), 1)
    partial_ref[...] = jnp.dot(
        spread,
        (at == slot).astype(jnp.float32),
        precision=lax.Precision.HIGHEST,
        preferred_element_type=jnp.float32,
    )


def term_of(hidden_ref, rows_ref, half):
    replicas, depth, chunk = rows_ref.shape
    rows = rows_ref[...].reshape(replicas * depth, chunk)
    lanes = slice(half * depth, (half + 1) * depth)
    hidden = jnp.concatenate([hidden_ref[p, :, lanes] for p in range(replicas)], axis=1)
    return jnp.dot(hidden, rows, preferred_element_type=jnp.float32)


def send_kernel(hidden_ref, rows_ref, product_ref, out_ref):
    chunk = rows_ref.shape[2]
    out_ref[:, :chunk] = term_of(hidden_ref, rows_ref, 0).astype(jnp.bfloat16)
    out_ref[:, chunk:] = product_ref[...]


def keep_kernel(hidden_ref, rows_ref, out_ref):
    out_ref[...] = term_of(hidden_ref, rows_ref, 1)


def finish_kernel(capacity, term_ref, product_ref, swapped_ref, weight_ref, hidden_ref):
    chunk = term_ref.shape[1]
    term = term_ref[...] + swapped_ref[:, :chunk].astype(jnp.float32)
    weight_ref[...] = term.astype(jnp.bfloat16)
    order = parity_order(hidden_ref.shape[1], capacity, False)
    both = jnp.concatenate([product_ref[...], swapped_ref[:, chunk:]], axis=1)
    moved = jnp.dot(both, order, preferred_element_type=jnp.float32)
    hidden_ref[...] = moved.astype(jnp.bfloat16)


def assign_slots(flat_ids, experts):
    expert_range = jnp.arange(experts, dtype=jnp.int32)
    onehot = (flat_ids[:, None] == expert_range[None, :]).astype(jnp.int32)
    earlier = jnp.cumsum(onehot, axis=0) - onehot
    return jnp.sum(earlier * onehot, axis=1)


def windows(n_dp, n_y, n_q, n_par, n_tensor):
    groups = []
    for dp in range(n_dp):
        for par in range(n_par):
            for run in range(n_tensor):
                group = []
                for y in range(n_y):
                    for q in range(n_q):
                        wraps = dp % 2 == 1 and q < n_q // 2
                        at = (run + 1) % n_tensor if wraps else run
                        group.append((((dp * n_y + y) * n_q + q) * n_par + par) * n_tensor + at)
                groups.append(group)
    return groups


def shards(cotangent, probs, expert_ids, saved_hidden, down_weight):
    n_y, n_q, n_par = lax.axis_size("y"), lax.axis_size("zq"), lax.axis_size("par")
    members = lax.axis_size("tensor")
    n_expert = n_y * n_q * n_par
    experts = n_y * n_q
    own_tokens, model_width = cotangent.shape
    hidden_cols = saved_hidden.shape[1]
    capacity = saved_hidden.shape[0] // n_expert

    n_dp = lax.axis_size("dp")
    chunk = model_width // n_dp
    half = experts * capacity
    swap = [(0, 1), (1, 0)]
    large = pltpu.CompilerParams(vmem_limit_bytes=60 << 20)
    small = pltpu.CompilerParams(vmem_limit_bytes=16 << 20)

    weight = down_weight.T
    vmem = pl.BlockSpec(memory_space=pltpu.VMEM)
    hbm = pl.BlockSpec(memory_space=pltpu.HBM)
    sent, hidden_mine = pl.pallas_call(
        functools.partial(prepare_kernel, capacity),
        in_specs=[hbm, vmem],
        out_specs=[vmem, vmem],
        out_shape=[
            jax.ShapeDtypeStruct((hidden_cols, chunk + half), jnp.bfloat16),
            jax.ShapeDtypeStruct((hidden_cols, half), jnp.bfloat16),
        ],
        scratch_shapes=[pltpu.SemaphoreType.DMA],
        compiler_params=large,
    )(weight, saved_hidden.T)
    swapped = lax.ppermute(sent, "par", swap)
    packed_width = model_width + PARTS * model_width // (PARTS + 1) + LANES
    packed = pl.pallas_call(
        pack_kernel,
        out_shape=jax.ShapeDtypeStruct((SUBLANES, packed_width), jnp.bfloat16),
        compiler_params=small,
    )(cotangent, probs.T)
    flat_ids = expert_ids.reshape(-1)
    keys = flat_ids * capacity + assign_slots(flat_ids, experts)
    start_row = lax.axis_index("tensor") * (own_tokens * 2)
    own_keys = lax.dynamic_slice_in_dim(keys, start_row, own_tokens * 2)
    packed, swapped, own_keys = lax.optimization_barrier((packed, swapped, own_keys))
    prefetched = lax.all_gather(jnp.concatenate([swapped, hidden_mine], axis=1), "dp", axis=0)

    gathered = lax.all_gather(packed, "tensor", axis=0)
    buffer = pl.pallas_call(
        functools.partial(fill_kernel, own_tokens, experts, capacity),
        out_shape=jax.ShapeDtypeStruct((half, model_width), jnp.bfloat16),
        compiler_params=pltpu.CompilerParams(vmem_limit_bytes=24 << 20),
    )(gathered, expert_ids.T)
    buffer = buffer.reshape(experts, capacity, model_width)
    groups = windows(n_dp, n_y, n_q, n_par, members)
    every = ("dp", "y", "zq", "par", "tensor")
    rows = lax.all_to_all(
        buffer, every, split_axis=0, concat_axis=0, axis_index_groups=groups, tiled=True
    ).reshape(half, model_width)

    product, product_theirs, partial_value, by_feature = pl.pallas_call(
        functools.partial(product_kernel, capacity),
        grid=(1,),
        in_specs=[
            vmem,
            hbm,
            hbm,
            vmem,
            pl.BlockSpec((hidden_cols, half), lambda i: (0, chunk // half)),
        ],
        out_specs=[vmem] * 4,
        out_shape=[
            jax.ShapeDtypeStruct((hidden_cols, half), jnp.bfloat16),
            jax.ShapeDtypeStruct((hidden_cols, half), jnp.bfloat16),
            jax.ShapeDtypeStruct((experts, LANES), jnp.float32),
            jax.ShapeDtypeStruct((n_dp, half, chunk), jnp.bfloat16),
        ],
        scratch_shapes=[
            pltpu.VMEM((hidden_cols, model_width), jnp.bfloat16),
            pltpu.VMEM((n_dp, hidden_cols, chunk), jnp.bfloat16),
            pltpu.VMEM((model_width, half), jnp.bfloat16),
            pltpu.SemaphoreType.DMA((2, 4)),
        ],
        compiler_params=pltpu.CompilerParams(vmem_limit_bytes=50 << 20),
    )(rows, weight, prefetched, hidden_mine, swapped)

    replica_rows = lax.all_to_all(by_feature, "dp", split_axis=0, concat_axis=0, tiled=True)
    partial_value = lax.psum(partial_value, "tensor")
    partial_value, replica_rows = lax.optimization_barrier((partial_value, replica_rows))
    term_cost = pl.CostEstimate(
        flops=2 * n_dp * half * hidden_cols * chunk,
        bytes_accessed=2 * n_dp * half * (hidden_cols + chunk) + 4 * hidden_cols * chunk,
        transcendentals=0,
    )
    medium = pltpu.CompilerParams(vmem_limit_bytes=50 << 20)
    saved = pl.BlockSpec((n_dp, hidden_cols, 2 * half), lambda i: (0, 0, chunk // (2 * half)))
    sent = pl.pallas_call(
        send_kernel,
        grid=(1,),
        in_specs=[saved, vmem, vmem],
        out_shape=jax.ShapeDtypeStruct((hidden_cols, chunk + half), jnp.bfloat16),
        cost_estimate=term_cost,
        compiler_params=medium,
    )(prefetched, replica_rows, product_theirs)
    swapped = lax.ppermute(sent, "par", swap)
    term = pl.pallas_call(
        keep_kernel,
        grid=(1,),
        in_specs=[saved, vmem],
        out_shape=jax.ShapeDtypeStruct((hidden_cols, chunk), jnp.float32),
        cost_estimate=term_cost,
        compiler_params=medium,
    )(prefetched, replica_rows)
    weight_grad, hidden_grad = pl.pallas_call(
        functools.partial(finish_kernel, capacity),
        out_shape=[
            jax.ShapeDtypeStruct((hidden_cols, chunk), jnp.bfloat16),
            jax.ShapeDtypeStruct((hidden_cols, 2 * half), jnp.bfloat16),
        ],
        compiler_params=medium,
    )(term, product, swapped)
    weight_grad, hidden_grad, own_keys = lax.optimization_barrier(
        (weight_grad, hidden_grad, own_keys)
    )
    weight_grad, hidden_grad = weight_grad.T, hidden_grad.T
    lookup = lax.all_to_all(
        partial_value, every, split_axis=0, concat_axis=0, axis_index_groups=groups, tiled=True
    )

    expert = lax.broadcasted_iota(jnp.int32, (1, experts, LANES), 1)
    slot = lax.broadcasted_iota(jnp.int32, (1, experts, LANES), 2)
    chosen = (own_keys[:, None, None] == expert * capacity + slot) & (slot < capacity)
    values = jnp.sum(jnp.where(chosen, lookup[None], 0.0), axis=(1, 2)).reshape(own_tokens, 2)
    prob_grad = values / probs
    return (hidden_grad, weight_grad, prob_grad)


def solution(mesh):
    n_dp, n_expert, n_tensor = mesh.devices.shape
    fine = Mesh(
        mesh.devices.reshape(n_dp, 4, n_expert // 8, 2, n_tensor), ("dp", "y", "zq", "par", "tensor")
    )
    expert = ("y", "zq", "par")
    in_specs = (
        P(("dp",) + expert + ("tensor",), None),
        P(("dp",) + expert + ("tensor",), None),
        P(("dp",) + expert, None),
        P("dp", expert + ("tensor",)),
        P(None, expert + ("tensor",)),
    )
    out_specs = (
        P("dp", expert + ("tensor",)),
        P("dp", expert + ("tensor",)),
        P(("dp",) + expert + ("tensor",), None),
    )
    return jax.shard_map(shards, mesh=fine, in_specs=in_specs, out_specs=out_specs, check_vma=False)
```

```python
import functools

import jax
import jax.numpy as jnp
from jax import lax
from jax.experimental import pallas as pl
from jax.experimental.pallas import tpu as pltpu
from jax.sharding import Mesh, PartitionSpec as P

LANES = 128
SUBLANES = 8
PARTS = 3


def split3(value):
    high = value.astype(jnp.bfloat16)
    rest = value - high.astype(jnp.float32)
    middle = rest.astype(jnp.bfloat16)
    low = (rest - middle.astype(jnp.float32)).astype(jnp.bfloat16)
    return high, middle, low


def pack_kernel(cot_ref, probs_ref, out_ref):
    own_tokens, width = cot_ref.shape
    rest = own_tokens - SUBLANES
    piece = width // (PARTS + 1)
    out_ref[:, :width] = cot_ref[:SUBLANES, :]
    row = lax.broadcasted_iota(jnp.int32, (SUBLANES, own_tokens), 0)
    token = lax.broadcasted_iota(jnp.int32, (SUBLANES, own_tokens), 1)
    body = ((row < rest) & (token == SUBLANES + row)).astype(jnp.bfloat16)
    last = cot_ref[:, PARTS * piece :]
    for k in range(PARTS):
        source = SUBLANES + (row - rest) * PARTS + k
        tail = ((row >= rest) & (token == source)).astype(jnp.bfloat16)
        moved = jnp.dot(
            body, cot_ref[:, k * piece : (k + 1) * piece], preferred_element_type=jnp.float32
        ) + jnp.dot(tail, last, preferred_element_type=jnp.float32)
        start = width + k * piece
        out_ref[:, start : start + piece] = moved.astype(jnp.bfloat16)
    place = lax.axis_index("tensor") * own_tokens
    lane = lax.broadcasted_iota(jnp.int32, (own_tokens, LANES), 1)
    owner = lax.broadcasted_iota(jnp.int32, (own_tokens, LANES), 0)
    here = (lane == owner + place).astype(jnp.bfloat16)
    parts = [
        jnp.dot(part, here, preferred_element_type=jnp.float32) for part in split3(probs_ref[...])
    ]
    meta = jnp.concatenate(parts + [jnp.zeros((SUBLANES - 2 * PARTS, LANES), jnp.float32)], axis=0)
    out_ref[:, width + PARTS * piece :] = meta.astype(jnp.bfloat16)


def fill_kernel(own_tokens, experts, capacity, gathered_ref, ids_ref, out_ref):
    members = gathered_ref.shape[0]
    width = out_ref.shape[1]
    group = members * own_tokens
    rest = own_tokens - SUBLANES
    piece = width // (PARTS + 1)
    block = members * SUBLANES
    lane = lax.broadcasted_iota(jnp.int32, (group, LANES), 1)
    token = lax.broadcasted_iota(jnp.int32, (group, LANES), 0)
    moved = jnp.dot(
        ids_ref[...].astype(jnp.float32).astype(jnp.bfloat16),
        (lane == token).astype(jnp.bfloat16),
        preferred_element_type=jnp.float32,
    ).astype(jnp.int32)
    real = lax.broadcasted_iota(jnp.int32, (1, LANES), 1) < group
    spread = [jnp.where(real, moved[k : k + 1], -1) for k in range(2)]
    expert = lax.broadcasted_iota(jnp.int32, (experts, LANES), 0)
    named = [(spread[k] == expert).astype(jnp.float32) for k in range(2)]
    first = lax.broadcasted_iota(jnp.int32, (LANES, LANES), 0)
    second = lax.broadcasted_iota(jnp.int32, (LANES, LANES), 1)
    earlier = jnp.dot(
        (named[0] + named[1]).astype(jnp.bfloat16),
        (first < second).astype(jnp.bfloat16),
        preferred_element_type=jnp.float32,
    )
    meta = gathered_ref[:, :, width + PARTS * piece :].astype(jnp.float32)
    meta = jnp.sum(meta, axis=0)
    row = lax.broadcasted_iota(jnp.int32, (experts * capacity, LANES), 0)
    selector = jnp.zeros((experts * capacity, LANES), jnp.float32)
    weight = jnp.zeros((experts * capacity, LANES), jnp.float32)
    for k in range(2):
        count = earlier if k == 0 else earlier + named[0]
        slot = jnp.sum(count * named[k], axis=0, keepdims=True).astype(jnp.int32)
        key = jnp.where(spread[k] >= 0, spread[k] * capacity + slot, -1)
        prob = meta[k : k + 1] + meta[2 + k : 3 + k] + meta[4 + k : 5 + k]
        match = row == key
        selector = jnp.where(match, 1.0, selector)
        weight = jnp.where(match, prob, weight)
    scale = jnp.sum(weight, axis=1, keepdims=True)
    selector = selector.astype(jnp.bfloat16)

    region, within = second // block, second % SUBLANES
    base = ((second % block) // SUBLANES) * own_tokens
    head = jnp.where(region == 0, base + within, -1)
    body = jnp.where((region == 1) & (within < rest), base + SUBLANES + within, head)
    tail = base + SUBLANES + (within - rest) * PARTS + region - 1
    tail = jnp.where((region >= 1) & (within >= rest), tail, head)

    def picked(source):
        moved = jnp.dot(
            selector, (first == source).astype(jnp.bfloat16), preferred_element_type=jnp.float32
        )
        return moved.astype(jnp.bfloat16)

    picked_body, picked_tail = picked(body)[:, : 2 * block], picked(tail)

    def rows_at(start, step):
        rows = gathered_ref[:, :, start : start + step].astype(jnp.float32)
        return rows.reshape(block, step)

    step = 512
    for start in range(0, width, step):
        found = [rows_at(start, step)]
        if start < PARTS * piece:
            found.append(rows_at(width + start, step))
            chosen = picked_body
        else:
            for k in range(PARTS):
                found.append(rows_at(width + k * piece + start - PARTS * piece, step))
            chosen = picked_tail
        rows = jnp.dot(
            chosen,
            jnp.concatenate(found, axis=0).astype(jnp.bfloat16),
            preferred_element_type=jnp.float32,
        )
        out_ref[:, start : start + step] = (rows * scale).astype(jnp.bfloat16)


def parity_order(rows, capacity, from_natural):
    lanes = rows // 2
    axes = (0, 1) if from_natural else (1, 0)
    natural = lax.broadcasted_iota(jnp.int32, (rows, rows), axes[0])
    ordered = lax.broadcasted_iota(jnp.int32, (rows, rows), axes[1])
    here = lax.axis_index("par")
    parity = jnp.where(ordered < lanes, here, 1 - here)
    within = ordered % lanes
    source = (within // capacity) * (2 * capacity) + parity * capacity + within % capacity
    return (natural == source).astype(jnp.bfloat16)


def prepare_kernel(capacity, chunk_ref, hidden_ref, send_ref, mine_ref):
    rows = hidden_ref.shape[1]
    chunk = chunk_ref.shape[1]
    send_ref[:, :chunk] = chunk_ref[...]
    order = parity_order(rows, capacity, True)
    moved = jnp.dot(hidden_ref[...], order, preferred_element_type=jnp.float32)
    moved = moved.astype(jnp.bfloat16)
    mine_ref[...] = moved[:, : rows // 2]
    send_ref[:, chunk:] = moved[:, rows // 2 :]


def product_kernel(
    capacity,
    rows_ref,
    weight_ref,
    weight_theirs_ref,
    hidden_ref,
    hidden_theirs_ref,
    mine_ref,
    theirs_ref,
    partial_ref,
    by_feature_ref,
    weight_buf,
    theirs_buf,
    turned,
    sems,
):
    replicas, cols, chunk = theirs_buf.shape
    cuts = (0, cols // 32 * 16, cols)
    weight_copies = [
        pltpu.make_async_copy(
            weight_ref.at[start:stop], weight_buf.at[start:stop], sems.at[0, index]
        )
        for index, (start, stop) in enumerate(zip(cuts[:-1], cuts[1:]))
    ]
    per = replicas // 4
    theirs_copies = [
        pltpu.make_async_copy(
            weight_theirs_ref.at[index * per : (index + 1) * per, :, :chunk],
            theirs_buf.at[index * per : (index + 1) * per],
            sems.at[1, index],
        )
        for index in range(4)
    ]
    for copy in theirs_copies + weight_copies:
        copy.start()
    for index in range(replicas):
        rows = rows_ref[:, index * chunk : (index + 1) * chunk]
        by_feature_ref[index] = rows
        turned[index * chunk : (index + 1) * chunk, :] = rows.T
    theirs = jnp.zeros(theirs_ref.shape, jnp.float32)
    for index in range(4):
        theirs_copies[index].wait()
        for replica in range(index * per, (index + 1) * per):
            theirs += jnp.dot(
                theirs_buf[replica],
                turned[replica * chunk : (replica + 1) * chunk, :],
                preferred_element_type=jnp.float32,
            )
    mine = []
    for index, (start, stop) in enumerate(zip(cuts[:-1], cuts[1:])):
        weight_copies[index].wait()
        mine.append(
            jnp.dot(weight_buf[start:stop], turned[...], preferred_element_type=jnp.float32)
        )
    mine = jnp.concatenate(mine, axis=0)
    mine_ref[...] = mine.astype(jnp.bfloat16)
    theirs_ref[...] = theirs.astype(jnp.bfloat16)
    summed = jnp.sum(
        hidden_ref[...].astype(jnp.float32) * mine
        + hidden_theirs_ref[...].astype(jnp.float32) * theirs,
        axis=0,
        keepdims=True,
    )
    lanes = summed.shape[1]
    experts = partial_ref.shape[0]
    of_expert = lax.broadcasted_iota(jnp.int32, (experts, lanes), 1) // capacity
    expert = lax.broadcasted_iota(jnp.int32, (experts, lanes), 0)
    spread = jnp.where(of_expert == expert, summed, 0.0)
    at = lax.broadcasted_iota(jnp.int32, (lanes, LANES), 0) % capacity
    slot = lax.broadcasted_iota(jnp.int32, (lanes, LANES), 1)
    partial_ref[...] = jnp.dot(
        spread,
        (at == slot).astype(jnp.float32),
        precision=lax.Precision.HIGHEST,
        preferred_element_type=jnp.float32,
    )


def term_of(hidden_ref, rows_ref, half):
    replicas, depth, chunk = rows_ref.shape
    rows = rows_ref[...].reshape(replicas * depth, chunk)
    lanes = slice(half * depth, (half + 1) * depth)
    hidden = jnp.concatenate([hidden_ref[p, :, lanes] for p in range(replicas)], axis=1)
    return jnp.dot(hidden, rows, preferred_element_type=jnp.float32)


def send_kernel(hidden_ref, rows_ref, product_ref, out_ref):
    chunk = rows_ref.shape[2]
    out_ref[:, :chunk] = term_of(hidden_ref, rows_ref, 0).astype(jnp.bfloat16)
    out_ref[:, chunk:] = product_ref[...]


def keep_kernel(hidden_ref, rows_ref, out_ref):
    out_ref[...] = term_of(hidden_ref, rows_ref, 1)


def finish_kernel(capacity, term_ref, product_ref, swapped_ref, weight_ref, hidden_ref):
    chunk = term_ref.shape[1]
    term = term_ref[...] + swapped_ref[:, :chunk].astype(jnp.float32)
    weight_ref[...] = term.astype(jnp.bfloat16)
    order = parity_order(hidden_ref.shape[1], capacity, False)
    both = jnp.concatenate([product_ref[...], swapped_ref[:, chunk:]], axis=1)
    moved = jnp.dot(both, order, preferred_element_type=jnp.float32)
    hidden_ref[...] = moved.astype(jnp.bfloat16)


def assign_slots(flat_ids, experts):
    expert_range = jnp.arange(experts, dtype=jnp.int32)
    onehot = (flat_ids[:, None] == expert_range[None, :]).astype(jnp.int32)
    earlier = jnp.cumsum(onehot, axis=0) - onehot
    return jnp.sum(earlier * onehot, axis=1)


def windows(n_dp, n_y, n_q, n_par, n_tensor):
    groups = []
    for dp in range(n_dp):
        for par in range(n_par):
            for run in range(n_tensor):
                group = []
                for y in range(n_y):
                    for q in range(n_q):
                        wraps = dp % 2 == 1 and q < n_q // 2
                        at = (run + 1) % n_tensor if wraps else run
                        group.append((((dp * n_y + y) * n_q + q) * n_par + par) * n_tensor + at)
                groups.append(group)
    return groups


def shards(cotangent, probs, expert_ids, saved_hidden, down_weight):
    n_y, n_q, n_par = lax.axis_size("y"), lax.axis_size("zq"), lax.axis_size("par")
    members = lax.axis_size("tensor")
    n_expert = n_y * n_q * n_par
    experts = n_y * n_q
    own_tokens, model_width = cotangent.shape
    hidden_cols = saved_hidden.shape[1]
    capacity = saved_hidden.shape[0] // n_expert

    n_dp = lax.axis_size("dp")
    chunk = model_width // n_dp
    half = experts * capacity
    swap = [(0, 1), (1, 0)]
    small = pltpu.CompilerParams(vmem_limit_bytes=16 << 20)

    weight = down_weight.T
    vmem = pl.BlockSpec(memory_space=pltpu.VMEM)
    hbm = pl.BlockSpec(memory_space=pltpu.HBM)
    sent, hidden_mine = pl.pallas_call(
        functools.partial(prepare_kernel, capacity),
        out_shape=[
            jax.ShapeDtypeStruct((hidden_cols, chunk + half), jnp.bfloat16),
            jax.ShapeDtypeStruct((hidden_cols, half), jnp.bfloat16),
        ],
        compiler_params=small,
    )(
        lax.dynamic_slice_in_dim(weight, lax.axis_index("dp") * chunk, chunk, axis=1),
        saved_hidden.T,
    )
    swapped = lax.ppermute(sent, "par", swap)
    packed_width = model_width + PARTS * model_width // (PARTS + 1) + LANES
    packed = pl.pallas_call(
        pack_kernel,
        out_shape=jax.ShapeDtypeStruct((SUBLANES, packed_width), jnp.bfloat16),
        compiler_params=small,
    )(cotangent, probs.T)
    flat_ids = expert_ids.reshape(-1)
    keys = flat_ids * capacity + assign_slots(flat_ids, experts)
    start_row = lax.axis_index("tensor") * (own_tokens * 2)
    own_keys = lax.dynamic_slice_in_dim(keys, start_row, own_tokens * 2)
    packed, swapped, own_keys = lax.optimization_barrier((packed, swapped, own_keys))
    prefetched = lax.all_gather(jnp.concatenate([swapped, hidden_mine], axis=1), "dp", axis=0)

    gathered = lax.all_gather(packed, "tensor", axis=0)
    buffer = pl.pallas_call(
        functools.partial(fill_kernel, own_tokens, experts, capacity),
        out_shape=jax.ShapeDtypeStruct((half, model_width), jnp.bfloat16),
        compiler_params=pltpu.CompilerParams(vmem_limit_bytes=24 << 20),
    )(gathered, expert_ids.T)
    buffer = buffer.reshape(experts, capacity, model_width)
    groups = windows(n_dp, n_y, n_q, n_par, members)
    every = ("dp", "y", "zq", "par", "tensor")
    rows = lax.all_to_all(
        buffer, every, split_axis=0, concat_axis=0, axis_index_groups=groups, tiled=True
    ).reshape(half, model_width)

    product, product_theirs, partial_value, by_feature = pl.pallas_call(
        functools.partial(product_kernel, capacity),
        grid=(1,),
        in_specs=[
            vmem,
            hbm,
            hbm,
            vmem,
            pl.BlockSpec((hidden_cols, half), lambda i: (0, chunk // half)),
        ],
        out_specs=[vmem] * 4,
        out_shape=[
            jax.ShapeDtypeStruct((hidden_cols, half), jnp.bfloat16),
            jax.ShapeDtypeStruct((hidden_cols, half), jnp.bfloat16),
            jax.ShapeDtypeStruct((experts, LANES), jnp.float32),
            jax.ShapeDtypeStruct((n_dp, half, chunk), jnp.bfloat16),
        ],
        scratch_shapes=[
            pltpu.VMEM((hidden_cols, model_width), jnp.bfloat16),
            pltpu.VMEM((n_dp, hidden_cols, chunk), jnp.bfloat16),
            pltpu.VMEM((model_width, half), jnp.bfloat16),
            pltpu.SemaphoreType.DMA((2, 4)),
        ],
        compiler_params=pltpu.CompilerParams(vmem_limit_bytes=50 << 20),
    )(rows, weight, prefetched, hidden_mine, swapped)

    replica_rows = lax.all_to_all(by_feature, "dp", split_axis=0, concat_axis=0, tiled=True)
    partial_value = lax.psum(partial_value, "tensor")
    partial_value, replica_rows = lax.optimization_barrier((partial_value, replica_rows))
    term_cost = pl.CostEstimate(
        flops=2 * n_dp * half * hidden_cols * chunk,
        bytes_accessed=2 * n_dp * half * (hidden_cols + chunk) + 4 * hidden_cols * chunk,
        transcendentals=0,
    )
    medium = pltpu.CompilerParams(vmem_limit_bytes=50 << 20)
    saved = pl.BlockSpec((n_dp, hidden_cols, 2 * half), lambda i: (0, 0, chunk // (2 * half)))
    sent = pl.pallas_call(
        send_kernel,
        grid=(1,),
        in_specs=[saved, vmem, vmem],
        out_shape=jax.ShapeDtypeStruct((hidden_cols, chunk + half), jnp.bfloat16),
        cost_estimate=term_cost,
        compiler_params=medium,
    )(prefetched, replica_rows, product_theirs)
    swapped = lax.ppermute(sent, "par", swap)
    term = pl.pallas_call(
        keep_kernel,
        grid=(1,),
        in_specs=[saved, vmem],
        out_shape=jax.ShapeDtypeStruct((hidden_cols, chunk), jnp.float32),
        cost_estimate=term_cost,
        compiler_params=medium,
    )(prefetched, replica_rows)
    weight_grad, hidden_grad = pl.pallas_call(
        functools.partial(finish_kernel, capacity),
        out_shape=[
            jax.ShapeDtypeStruct((hidden_cols, chunk), jnp.bfloat16),
            jax.ShapeDtypeStruct((hidden_cols, 2 * half), jnp.bfloat16),
        ],
        compiler_params=medium,
    )(term, product, swapped)
    weight_grad, hidden_grad, own_keys = lax.optimization_barrier(
        (weight_grad, hidden_grad, own_keys)
    )
    weight_grad, hidden_grad = weight_grad.T, hidden_grad.T
    lookup = lax.all_to_all(
        partial_value, every, split_axis=0, concat_axis=0, axis_index_groups=groups, tiled=True
    )

    expert = lax.broadcasted_iota(jnp.int32, (1, experts, LANES), 1)
    slot = lax.broadcasted_iota(jnp.int32, (1, experts, LANES), 2)
    chosen = (own_keys[:, None, None] == expert * capacity + slot) & (slot < capacity)
    values = jnp.sum(jnp.where(chosen, lookup[None], 0.0), axis=(1, 2)).reshape(own_tokens, 2)
    prob_grad = values / probs
    return (hidden_grad, weight_grad, prob_grad)


def solution(mesh):
    n_dp, n_expert, n_tensor = mesh.devices.shape
    fine = Mesh(
        mesh.devices.reshape(n_dp, 4, n_expert // 8, 2, n_tensor), ("dp", "y", "zq", "par", "tensor")
    )
    expert = ("y", "zq", "par")
    in_specs = (
        P(("dp",) + expert + ("tensor",), None),
        P(("dp",) + expert + ("tensor",), None),
        P(("dp",) + expert, None),
        P("dp", expert + ("tensor",)),
        P(None, expert + ("tensor",)),
    )
    out_specs = (
        P("dp", expert + ("tensor",)),
        P("dp", expert + ("tensor",)),
        P(("dp",) + expert + ("tensor",), None),
    )
    return jax.shard_map(shards, mesh=fine, in_specs=in_specs, out_specs=out_specs, check_vma=False)
```

```python
import functools

import jax
import jax.numpy as jnp
from jax import lax
from jax.experimental import pallas as pl
from jax.experimental.pallas import tpu as pltpu
from jax.sharding import Mesh, PartitionSpec as P

LANES = 128
SUBLANES = 8
PARTS = 3


def split3(value):
    high = value.astype(jnp.bfloat16)
    rest = value - high.astype(jnp.float32)
    middle = rest.astype(jnp.bfloat16)
    low = (rest - middle.astype(jnp.float32)).astype(jnp.bfloat16)
    return high, middle, low


def pack_kernel(cot_ref, probs_ref, out_ref):
    own_tokens, width = cot_ref.shape
    rest = own_tokens - SUBLANES
    piece = width // (PARTS + 1)
    out_ref[:, :width] = cot_ref[:SUBLANES, :]
    row = lax.broadcasted_iota(jnp.int32, (SUBLANES, own_tokens), 0)
    token = lax.broadcasted_iota(jnp.int32, (SUBLANES, own_tokens), 1)
    body = ((row < rest) & (token == SUBLANES + row)).astype(jnp.bfloat16)
    last = cot_ref[:, PARTS * piece :]
    for k in range(PARTS):
        source = SUBLANES + (row - rest) * PARTS + k
        tail = ((row >= rest) & (token == source)).astype(jnp.bfloat16)
        moved = jnp.dot(
            body, cot_ref[:, k * piece : (k + 1) * piece], preferred_element_type=jnp.float32
        ) + jnp.dot(tail, last, preferred_element_type=jnp.float32)
        start = width + k * piece
        out_ref[:, start : start + piece] = moved.astype(jnp.bfloat16)
    place = lax.axis_index("tensor") * own_tokens
    lane = lax.broadcasted_iota(jnp.int32, (own_tokens, LANES), 1)
    owner = lax.broadcasted_iota(jnp.int32, (own_tokens, LANES), 0)
    here = (lane == owner + place).astype(jnp.bfloat16)
    parts = [
        jnp.dot(part, here, preferred_element_type=jnp.float32) for part in split3(probs_ref[...])
    ]
    meta = jnp.concatenate(parts + [jnp.zeros((SUBLANES - 2 * PARTS, LANES), jnp.float32)], axis=0)
    out_ref[:, width + PARTS * piece :] = meta.astype(jnp.bfloat16)


def fill_kernel(own_tokens, experts, capacity, gathered_ref, ids_ref, out_ref):
    members = gathered_ref.shape[0]
    width = out_ref.shape[1]
    group = members * own_tokens
    rest = own_tokens - SUBLANES
    piece = width // (PARTS + 1)
    block = members * SUBLANES
    lane = lax.broadcasted_iota(jnp.int32, (group, LANES), 1)
    token = lax.broadcasted_iota(jnp.int32, (group, LANES), 0)
    moved = jnp.dot(
        ids_ref[...].astype(jnp.float32).astype(jnp.bfloat16),
        (lane == token).astype(jnp.bfloat16),
        preferred_element_type=jnp.float32,
    ).astype(jnp.int32)
    real = lax.broadcasted_iota(jnp.int32, (1, LANES), 1) < group
    spread = [jnp.where(real, moved[k : k + 1], -1) for k in range(2)]
    expert = lax.broadcasted_iota(jnp.int32, (experts, LANES), 0)
    named = [(spread[k] == expert).astype(jnp.float32) for k in range(2)]
    first = lax.broadcasted_iota(jnp.int32, (LANES, LANES), 0)
    second = lax.broadcasted_iota(jnp.int32, (LANES, LANES), 1)
    earlier = jnp.dot(
        (named[0] + named[1]).astype(jnp.bfloat16),
        (first < second).astype(jnp.bfloat16),
        preferred_element_type=jnp.float32,
    )
    meta = gathered_ref[:, :, width + PARTS * piece :].astype(jnp.float32)
    meta = jnp.sum(meta, axis=0)
    row = lax.broadcasted_iota(jnp.int32, (experts * capacity, LANES), 0)
    selector = jnp.zeros((experts * capacity, LANES), jnp.float32)
    weight = jnp.zeros((experts * capacity, LANES), jnp.float32)
    for k in range(2):
        count = earlier if k == 0 else earlier + named[0]
        slot = jnp.sum(count * named[k], axis=0, keepdims=True).astype(jnp.int32)
        key = jnp.where(spread[k] >= 0, spread[k] * capacity + slot, -1)
        prob = meta[k : k + 1] + meta[2 + k : 3 + k] + meta[4 + k : 5 + k]
        match = row == key
        selector = jnp.where(match, 1.0, selector)
        weight = jnp.where(match, prob, weight)
    scale = jnp.sum(weight, axis=1, keepdims=True)
    selector = selector.astype(jnp.bfloat16)

    region, within = second // block, second % SUBLANES
    base = ((second % block) // SUBLANES) * own_tokens
    head = jnp.where(region == 0, base + within, -1)
    body = jnp.where((region == 1) & (within < rest), base + SUBLANES + within, head)
    tail = base + SUBLANES + (within - rest) * PARTS + region - 1
    tail = jnp.where((region >= 1) & (within >= rest), tail, head)

    def picked(source):
        moved = jnp.dot(
            selector, (first == source).astype(jnp.bfloat16), preferred_element_type=jnp.float32
        )
        return moved.astype(jnp.bfloat16)

    picked_body, picked_tail = picked(body)[:, : 2 * block], picked(tail)

    def rows_at(start, step):
        rows = gathered_ref[:, :, start : start + step].astype(jnp.float32)
        return rows.reshape(block, step)

    step = 512
    for start in range(0, width, step):
        found = [rows_at(start, step)]
        if start < PARTS * piece:
            found.append(rows_at(width + start, step))
            chosen = picked_body
        else:
            for k in range(PARTS):
                found.append(rows_at(width + k * piece + start - PARTS * piece, step))
            chosen = picked_tail
        rows = jnp.dot(
            chosen,
            jnp.concatenate(found, axis=0).astype(jnp.bfloat16),
            preferred_element_type=jnp.float32,
        )
        out_ref[:, start : start + step] = (rows * scale).astype(jnp.bfloat16)


def parity_order(rows, capacity, from_natural):
    lanes = rows // 2
    axes = (0, 1) if from_natural else (1, 0)
    natural = lax.broadcasted_iota(jnp.int32, (rows, rows), axes[0])
    ordered = lax.broadcasted_iota(jnp.int32, (rows, rows), axes[1])
    here = lax.axis_index("par")
    parity = jnp.where(ordered < lanes, here, 1 - here)
    within = ordered % lanes
    source = (within // capacity) * (2 * capacity) + parity * capacity + within % capacity
    return (natural == source).astype(jnp.bfloat16)


def sort_kernel(capacity, hidden_ref, mine_ref, send_ref):
    rows = hidden_ref.shape[1]
    order = parity_order(rows, capacity, True)
    moved = jnp.dot(hidden_ref[...], order, preferred_element_type=jnp.float32)
    moved = moved.astype(jnp.bfloat16)
    mine_ref[...] = moved[:, : rows // 2]
    send_ref[...] = moved[:, rows // 2 :]


def product_kernel(
    capacity,
    rows_ref,
    weight_ref,
    weight_theirs_ref,
    hidden_ref,
    hidden_theirs_ref,
    mine_ref,
    theirs_ref,
    partial_ref,
    by_feature_ref,
    weight_buf,
    theirs_buf,
    turned,
    sems,
):
    replicas, cols, chunk = theirs_buf.shape
    cuts = (0, cols // 32 * 16, cols)
    weight_copies = [
        pltpu.make_async_copy(
            weight_ref.at[start:stop], weight_buf.at[start:stop], sems.at[0, index]
        )
        for index, (start, stop) in enumerate(zip(cuts[:-1], cuts[1:]))
    ]
    per = replicas // 4
    theirs_copies = [
        pltpu.make_async_copy(
            weight_theirs_ref.at[index * per : (index + 1) * per, :, :chunk],
            theirs_buf.at[index * per : (index + 1) * per],
            sems.at[1, index],
        )
        for index in range(4)
    ]
    for copy in theirs_copies + weight_copies:
        copy.start()
    for index in range(replicas):
        rows = rows_ref[:, index * chunk : (index + 1) * chunk]
        by_feature_ref[index] = rows
        turned[index * chunk : (index + 1) * chunk, :] = rows.T
    theirs = jnp.zeros(theirs_ref.shape, jnp.float32)
    for index in range(4):
        theirs_copies[index].wait()
        for replica in range(index * per, (index + 1) * per):
            theirs += jnp.dot(
                theirs_buf[replica],
                turned[replica * chunk : (replica + 1) * chunk, :],
                preferred_element_type=jnp.float32,
            )
    mine = []
    for index, (start, stop) in enumerate(zip(cuts[:-1], cuts[1:])):
        weight_copies[index].wait()
        mine.append(
            jnp.dot(weight_buf[start:stop], turned[...], preferred_element_type=jnp.float32)
        )
    mine = jnp.concatenate(mine, axis=0)
    mine_ref[...] = mine.astype(jnp.bfloat16)
    theirs_ref[...] = theirs.astype(jnp.bfloat16)
    summed = jnp.sum(
        hidden_ref[...].astype(jnp.float32) * mine
        + hidden_theirs_ref[...].astype(jnp.float32) * theirs,
        axis=0,
        keepdims=True,
    )
    lanes = summed.shape[1]
    experts = partial_ref.shape[0]
    of_expert = lax.broadcasted_iota(jnp.int32, (experts, lanes), 1) // capacity
    expert = lax.broadcasted_iota(jnp.int32, (experts, lanes), 0)
    spread = jnp.where(of_expert == expert, summed, 0.0)
    at = lax.broadcasted_iota(jnp.int32, (lanes, LANES), 0) % capacity
    slot = lax.broadcasted_iota(jnp.int32, (lanes, LANES), 1)
    partial_ref[...] = jnp.dot(
        spread,
        (at == slot).astype(jnp.float32),
        precision=lax.Precision.HIGHEST,
        preferred_element_type=jnp.float32,
    )


def term_of(hidden_ref, rows_ref, half):
    replicas, depth, chunk = rows_ref.shape
    rows = rows_ref[...].reshape(replicas * depth, chunk)
    lanes = slice(half * depth, (half + 1) * depth)
    hidden = jnp.concatenate([hidden_ref[p, :, lanes] for p in range(replicas)], axis=1)
    return jnp.dot(hidden, rows, preferred_element_type=jnp.float32)


def send_kernel(hidden_ref, rows_ref, product_ref, out_ref):
    chunk = rows_ref.shape[2]
    out_ref[:, :chunk] = term_of(hidden_ref, rows_ref, 0).astype(jnp.bfloat16)
    out_ref[:, chunk:] = product_ref[...]


def keep_kernel(hidden_ref, rows_ref, out_ref):
    out_ref[...] = term_of(hidden_ref, rows_ref, 1)


def finish_kernel(capacity, term_ref, product_ref, swapped_ref, weight_ref, hidden_ref):
    chunk = term_ref.shape[1]
    term = term_ref[...] + swapped_ref[:, :chunk].astype(jnp.float32)
    weight_ref[...] = term.astype(jnp.bfloat16)
    order = parity_order(hidden_ref.shape[1], capacity, False)
    both = jnp.concatenate([product_ref[...], swapped_ref[:, chunk:]], axis=1)
    moved = jnp.dot(both, order, preferred_element_type=jnp.float32)
    hidden_ref[...] = moved.astype(jnp.bfloat16)


def assign_slots(flat_ids, experts):
    expert_range = jnp.arange(experts, dtype=jnp.int32)
    onehot = (flat_ids[:, None] == expert_range[None, :]).astype(jnp.int32)
    earlier = jnp.cumsum(onehot, axis=0) - onehot
    return jnp.sum(earlier * onehot, axis=1)


def windows(n_dp, n_y, n_q, n_par, n_tensor):
    groups = []
    for dp in range(n_dp):
        for par in range(n_par):
            for run in range(n_tensor):
                group = []
                for y in range(n_y):
                    for q in range(n_q):
                        wraps = dp % 2 == 1 and q < n_q // 2
                        at = (run + 1) % n_tensor if wraps else run
                        group.append((((dp * n_y + y) * n_q + q) * n_par + par) * n_tensor + at)
                groups.append(group)
    return groups


def shards(cotangent, probs, expert_ids, saved_hidden, down_weight):
    n_y, n_q, n_par = lax.axis_size("y"), lax.axis_size("zq"), lax.axis_size("par")
    members = lax.axis_size("tensor")
    n_expert = n_y * n_q * n_par
    experts = n_y * n_q
    own_tokens, model_width = cotangent.shape
    hidden_cols = saved_hidden.shape[1]
    capacity = saved_hidden.shape[0] // n_expert

    n_dp = lax.axis_size("dp")
    chunk = model_width // n_dp
    half = experts * capacity
    swap = [(0, 1), (1, 0)]
    small = pltpu.CompilerParams(vmem_limit_bytes=16 << 20)

    weight = down_weight.T
    vmem = pl.BlockSpec(memory_space=pltpu.VMEM)
    hbm = pl.BlockSpec(memory_space=pltpu.HBM)
    weight_sent = lax.dynamic_slice_in_dim(weight, lax.axis_index("dp") * chunk, chunk, axis=1)
    weight_swapped = lax.ppermute(weight_sent, "par", swap)
    hidden_mine, hidden_sent = pl.pallas_call(
        functools.partial(sort_kernel, capacity),
        out_shape=[jax.ShapeDtypeStruct((hidden_cols, half), jnp.bfloat16)] * 2,
        compiler_params=small,
    )(saved_hidden.T)
    hidden_theirs = lax.ppermute(hidden_sent, "par", swap)
    packed_width = model_width + PARTS * model_width // (PARTS + 1) + LANES
    packed = pl.pallas_call(
        pack_kernel,
        out_shape=jax.ShapeDtypeStruct((SUBLANES, packed_width), jnp.bfloat16),
        compiler_params=small,
    )(cotangent, probs.T)
    flat_ids = expert_ids.reshape(-1)
    keys = flat_ids * capacity + assign_slots(flat_ids, experts)
    start_row = lax.axis_index("tensor") * (own_tokens * 2)
    own_keys = lax.dynamic_slice_in_dim(keys, start_row, own_tokens * 2)
    packed, weight_swapped, hidden_theirs, own_keys = lax.optimization_barrier(
        (packed, weight_swapped, hidden_theirs, own_keys)
    )
    fetched = jnp.concatenate([weight_swapped, hidden_theirs, hidden_mine], axis=1)
    prefetched = lax.all_gather(fetched, "dp", axis=0)

    gathered = lax.all_gather(packed, "tensor", axis=0)
    buffer = pl.pallas_call(
        functools.partial(fill_kernel, own_tokens, experts, capacity),
        out_shape=jax.ShapeDtypeStruct((half, model_width), jnp.bfloat16),
        compiler_params=pltpu.CompilerParams(vmem_limit_bytes=24 << 20),
    )(gathered, expert_ids.T)
    buffer = buffer.reshape(experts, capacity, model_width)
    groups = windows(n_dp, n_y, n_q, n_par, members)
    every = ("dp", "y", "zq", "par", "tensor")
    rows = lax.all_to_all(
        buffer, every, split_axis=0, concat_axis=0, axis_index_groups=groups, tiled=True
    ).reshape(half, model_width)

    product, product_theirs, partial_value, by_feature = pl.pallas_call(
        functools.partial(product_kernel, capacity),
        grid=(1,),
        in_specs=[
            vmem,
            hbm,
            hbm,
            vmem,
            vmem,
        ],
        out_specs=[vmem] * 4,
        out_shape=[
            jax.ShapeDtypeStruct((hidden_cols, half), jnp.bfloat16),
            jax.ShapeDtypeStruct((hidden_cols, half), jnp.bfloat16),
            jax.ShapeDtypeStruct((experts, LANES), jnp.float32),
            jax.ShapeDtypeStruct((n_dp, half, chunk), jnp.bfloat16),
        ],
        scratch_shapes=[
            pltpu.VMEM((hidden_cols, model_width), jnp.bfloat16),
            pltpu.VMEM((n_dp, hidden_cols, chunk), jnp.bfloat16),
            pltpu.VMEM((model_width, half), jnp.bfloat16),
            pltpu.SemaphoreType.DMA((2, 4)),
        ],
        compiler_params=pltpu.CompilerParams(vmem_limit_bytes=50 << 20),
    )(rows, weight, prefetched, hidden_mine, hidden_theirs)

    replica_rows = lax.all_to_all(by_feature, "dp", split_axis=0, concat_axis=0, tiled=True)
    partial_value = lax.psum(partial_value, "tensor")
    partial_value, replica_rows = lax.optimization_barrier((partial_value, replica_rows))
    term_cost = pl.CostEstimate(
        flops=2 * n_dp * half * hidden_cols * chunk,
        bytes_accessed=2 * n_dp * half * (hidden_cols + chunk) + 4 * hidden_cols * chunk,
        transcendentals=0,
    )
    medium = pltpu.CompilerParams(vmem_limit_bytes=50 << 20)
    saved = pl.BlockSpec((n_dp, hidden_cols, 2 * half), lambda i: (0, 0, chunk // (2 * half)))
    sent = pl.pallas_call(
        send_kernel,
        grid=(1,),
        in_specs=[saved, vmem, vmem],
        out_shape=jax.ShapeDtypeStruct((hidden_cols, chunk + half), jnp.bfloat16),
        cost_estimate=term_cost,
        compiler_params=medium,
    )(prefetched, replica_rows, product_theirs)
    swapped = lax.ppermute(sent, "par", swap)
    term = pl.pallas_call(
        keep_kernel,
        grid=(1,),
        in_specs=[saved, vmem],
        out_shape=jax.ShapeDtypeStruct((hidden_cols, chunk), jnp.float32),
        cost_estimate=term_cost,
        compiler_params=medium,
    )(prefetched, replica_rows)
    weight_grad, hidden_grad = pl.pallas_call(
        functools.partial(finish_kernel, capacity),
        out_shape=[
            jax.ShapeDtypeStruct((hidden_cols, chunk), jnp.bfloat16),
            jax.ShapeDtypeStruct((hidden_cols, 2 * half), jnp.bfloat16),
        ],
        compiler_params=medium,
    )(term, product, swapped)
    weight_grad, hidden_grad, own_keys = lax.optimization_barrier(
        (weight_grad, hidden_grad, own_keys)
    )
    weight_grad, hidden_grad = weight_grad.T, hidden_grad.T
    lookup = lax.all_to_all(
        partial_value, every, split_axis=0, concat_axis=0, axis_index_groups=groups, tiled=True
    )

    expert = lax.broadcasted_iota(jnp.int32, (1, experts, LANES), 1)
    slot = lax.broadcasted_iota(jnp.int32, (1, experts, LANES), 2)
    chosen = (own_keys[:, None, None] == expert * capacity + slot) & (slot < capacity)
    values = jnp.sum(jnp.where(chosen, lookup[None], 0.0), axis=(1, 2)).reshape(own_tokens, 2)
    prob_grad = values / probs
    return (hidden_grad, weight_grad, prob_grad)


def solution(mesh):
    n_dp, n_expert, n_tensor = mesh.devices.shape
    fine = Mesh(
        mesh.devices.reshape(n_dp, 4, n_expert // 8, 2, n_tensor), ("dp", "y", "zq", "par", "tensor")
    )
    expert = ("y", "zq", "par")
    in_specs = (
        P(("dp",) + expert + ("tensor",), None),
        P(("dp",) + expert + ("tensor",), None),
        P(("dp",) + expert, None),
        P("dp", expert + ("tensor",)),
        P(None, expert + ("tensor",)),
    )
    out_specs = (
        P("dp", expert + ("tensor",)),
        P("dp", expert + ("tensor",)),
        P(("dp",) + expert + ("tensor",), None),
    )
    return jax.shard_map(shards, mesh=fine, in_specs=in_specs, out_specs=out_specs, check_vma=False)
```
